32 devices in a mesh: dom: 8 (over z, y), col: 4 (over x, core).
Axes of the slice: x: 2, y: 2, z: 4, core: 2. Of those that a mesh axis runs over, the one named last changes fastest.
Arguments:
- embeddings: bfloat16 [2, 200, 32768], P(None, 'col', 'dom'), may hold values from -3 to 3
- relations: bfloat16 [2, 200, 512], P(None, 'col'), may hold values from -3 to 3
- source_ids: int32 [4, 8192], P(None, 'dom'), may hold values from 0 to 4095
- relation_ids: int32 [4, 8192], P(None, 'dom'), may hold values from 0 to 511
- target_ids: int32 [4, 8192], P(None, 'dom'), may hold values from 0 to 4095
- negative_ids: int32 [4, 32, 256], P(None, 'dom'), may hold values from 0 to 127
- served_rows: int32 [64, 16], P('dom'), may hold values from 0 to 4095
Outputs:
- entity_grad: float32 [2, 200, 32768], P(None, 'col', 'dom')
The draws below stay inside these ranges and needn't reach their ends.
All inputs are finite; a program needn't handle non-finite values.
Results may differ from the reference program's by a relative error of at most 0.007.
Values may be sent and summed in bfloat16 or wider, within the bound.
No kernel may reach another device: no remote copies, remote signals or barrier semaphores. Data moves between devices by JAX's collectives and lax.ppermute only.
A program may use at most 128 MiB of HBM per device.

```python
import math
import jax
import jax.numpy as jnp
import numpy as np
from jax import lax

DIM = 200
RELS = 512
ENT_DEV = 4096
E_DEV = 1024
CH = 256
NCH = 256
NB = 4
CAP = 16
ENTS = 32768
EDGES = 8192
SPANS = 4
POOL = 128
N_DOM = 8
N_COL = 4


def plant(entries, stream_key, smallest, top_value):
    longest = entries.shape.index(max(entries.shape))
    spots = []
    for shift in (0, 1):
        where = [jax.random.randint(jax.random.fold_in(stream_key, axis), (), 0, length) for axis, length in enumerate(entries.shape)]
        where[longest] = (where[longest] + shift) % entries.shape[longest]
        spots.append(tuple(where))
    return entries.at[spots[0]].set(smallest).at[spots[1]].set(top_value)


def level_of(own_key, shape, cuts, least, largest):
    factor_of, own = 1.0, jax.random.fold_in(own_key, 6)
    for dim, blocks in cuts:
        steps = jnp.exp(jax.random.uniform(jax.random.fold_in(own, dim), (blocks,), jnp.float32, least / len(cuts), largest / len(cuts)))
        factor_of = factor_of * jnp.repeat(steps, shape[dim] // blocks).reshape([-1 if axis == dim else 1 for axis in range(len(shape))])
    return factor_of


def rank_table(count, skew):
    loads = [(1 << 20) // math.isqrt(rank ** skew) + 1 for rank in range(1, count + 1)]
    spread = 1 + sum(loads) // (1 << 30)
    return np.cumsum(np.array([max(1, weight // spread) for weight in loads]))


def ranked_ids(stream_key, dims, number_of, slope):
    grid = rank_table(number_of, slope)
    lot = jax.random.randint(jax.random.fold_in(stream_key, 1), dims, 0, int(grid[number_of - 1]))
    grade = jnp.searchsorted(jnp.asarray(grid, jnp.int32), lot, side="right")
    return jax.random.permutation(jax.random.fold_in(stream_key, 2), number_of)[grade].astype(jnp.int32)


def gaussian(own_key, extent, deviation, bound, split=(), dtype=jnp.bfloat16):
    values = jax.random.normal(own_key, extent, jnp.float32) * deviation
    if len(split) > 0:
        values = level_of(own_key, extent, split, -0.22, 0.18) * values
    return jnp.clip(values, min=-bound, max=bound).astype(dtype)


def setup_inputs(seed: int = 0) -> dict:
    key_of = jax.random.split(jax.random.key(seed), 8)
    embeddings = gaussian(key_of[0], (2, DIM, ENTS), 0.5, 3.0, ((1, 4), (2, 8)))
    relations = gaussian(key_of[1], (2, DIM, RELS), 0.5, 3.0, ((1, 4),))
    source_ids = plant(jax.random.randint(key_of[2], (NB, EDGES), 0, ENT_DEV), jax.random.fold_in(key_of[2], 1), 0, ENT_DEV - 1).astype(jnp.int32)
    relation_ids = plant(ranked_ids(key_of[3], (NB, EDGES), RELS, 2), jax.random.fold_in(key_of[3], 3), 0, RELS - 1).astype(jnp.int32)
    target_ids = plant(ranked_ids(key_of[4], (NB, EDGES), ENT_DEV, 1), jax.random.fold_in(key_of[4], 3), 0, ENT_DEV - 1).astype(jnp.int32)
    negative_ids = plant(ranked_ids(key_of[5], (NB, SPANS * N_DOM, NCH), POOL, 1), jax.random.fold_in(key_of[5], 3), 0, POOL - 1).astype(jnp.int32)
    served_rows = plant(jax.random.randint(key_of[6], (N_DOM * N_DOM, CAP), 0, ENT_DEV), jax.random.fold_in(key_of[6], 1), 0, ENT_DEV - 1).astype(jnp.int32)
    return dict(embeddings=embeddings, relations=relations, source_ids=source_ids, relation_ids=relation_ids, target_ids=target_ids, negative_ids=negative_ids, served_rows=served_rows)


def partition_step(inputs):
    table_part, target_part, pool_part, sources, relation_rows, targets, negatives = inputs
    group_width = DIM // N_COL
    highest = lax.Precision.HIGHEST
    source_rows = table_part[:, :, sources].astype(jnp.float32)
    relation_vals = relation_rows.astype(jnp.float32)
    target_rows = target_part[:, :, targets].astype(jnp.float32)
    product = jnp.stack([source_rows[0] * relation_vals[0] - source_rows[1] * relation_vals[1],
                         source_rows[0] * relation_vals[1] + source_rows[1] * relation_vals[0]])
    rounded = lax.optimization_barrier(product.astype(jnp.bfloat16)).astype(jnp.float32)
    positive_cols = jnp.sum((rounded * target_rows).reshape(2, N_COL, group_width, E_DEV), axis=(0, 2))
    positive = jnp.sum(lax.optimization_barrier(positive_cols.astype(jnp.bfloat16)).astype(jnp.float32), axis=0)
    negative_rows = pool_part[:, :, negatives.reshape(-1)].astype(jnp.float32).reshape(2, DIM, SPANS, NCH)
    query_cols = rounded.reshape(2, N_COL, group_width, SPANS, CH)
    negative_groups = negative_rows.reshape(2, N_COL, group_width, SPANS, NCH)
    negative_cols = jnp.einsum('acdjh,acdjn->cjhn', query_cols, negative_groups, precision=highest)
    negative = jnp.sum(lax.optimization_barrier(negative_cols.astype(jnp.bfloat16)).astype(jnp.float32), axis=0)
    positive_slope = -jax.nn.sigmoid(-positive)
    negative_slope = lax.optimization_barrier(jax.nn.sigmoid(negative).astype(jnp.bfloat16)).astype(jnp.float32)
    query_rows = rounded.reshape(2, DIM, SPANS, CH)
    pool_terms = jnp.einsum('jhn,adjh->adjn', negative_slope, query_rows, precision=highest)
    pool_grad = jnp.zeros((2, DIM, POOL), jnp.float32).at[:, :, negatives.reshape(-1)].add(
        pool_terms.reshape(2, DIM, SPANS * NCH))
    query_terms = jnp.einsum('jhn,adjn->adjh', negative_slope, negative_rows, precision=highest).reshape(2, DIM, E_DEV)
    total = positive_slope * target_rows + query_terms
    source_grad = jnp.stack([total[0] * relation_vals[0] + total[1] * relation_vals[1],
                             total[1] * relation_vals[0] - total[0] * relation_vals[1]])
    source_full = jnp.zeros((2, DIM, ENT_DEV), jnp.float32).at[:, :, sources].add(source_grad)
    target_full = jnp.zeros((2, DIM, ENT_DEV), jnp.float32).at[:, :, targets].add(positive_slope * rounded)
    return source_full, target_full, pool_grad


def add_owned(gradient, indices, values):
    return gradient.at[:, :, indices].add(values)


def reference(embeddings, relations, source_ids, relation_ids, target_ids, negative_ids, served_rows):
    table = embeddings.reshape(2, DIM, N_DOM, ENT_DEV)
    served = served_rows.reshape(N_DOM, N_DOM * CAP)
    fetched = jnp.take_along_axis(table, served[None, None], axis=3)
    negative_pool = fetched.reshape(2, DIM, N_DOM, N_DOM, CAP).transpose(0, 1, 3, 2, 4).reshape(2, DIM, N_DOM, POOL)
    by_owner = jnp.moveaxis(table, 2, 0)
    pools = jnp.moveaxis(negative_pool, 2, 0)
    entity_sum = jnp.zeros((N_DOM, 2, DIM, ENT_DEV), jnp.float32)
    pool_sum = jnp.zeros((N_DOM, 2, DIM, POOL), jnp.float32)
    for bucket in range(NB):
        targets_block = jnp.roll(by_owner, bucket, axis=0)
        sources = source_ids[bucket].reshape(N_DOM, E_DEV)
        targets = target_ids[bucket].reshape(N_DOM, E_DEV)
        relation_rows = jnp.moveaxis(relations[:, :, relation_ids[bucket]].reshape(2, DIM, N_DOM, E_DEV), 2, 0)
        negatives = negative_ids[bucket].reshape(N_DOM, SPANS, NCH)
        source_terms, target_terms, pool_terms = lax.map(
            partition_step, (by_owner, targets_block, pools, sources, relation_rows, targets, negatives))
        entity_sum = entity_sum + source_terms + jnp.roll(target_terms, -bucket, axis=0)
        pool_sum = pool_sum + pool_terms
    returned = pool_sum.reshape(N_DOM, 2, DIM, N_DOM, CAP).transpose(3, 1, 2, 0, 4).reshape(N_DOM, 2, DIM, N_DOM * CAP)
    owned = jax.vmap(add_owned)(entity_sum, served, returned)
    return jnp.moveaxis(owned, 0, 2).reshape(2, DIM, ENTS)
```

```python
import functools

import jax
import jax.numpy as jnp
from jax import lax
from jax.experimental import pallas as pl
from jax.experimental.pallas import tpu as pltpu
from jax.sharding import PartitionSpec as P

BF16 = jnp.bfloat16
F32 = jnp.float32
I32 = jnp.int32
LANES = 128
PACK = 16
TILE = 256
VMEM_BYTES = 56 << 20


def rotate(shard, axis, by):
    size = lax.axis_size(axis)
    return lax.ppermute(shard, axis, [(i, (i + by) % size) for i in range(size)])


def swap(shard, axis, bit):
    size = lax.axis_size(axis)
    return lax.ppermute(shard, axis, [(i, i ^ bit) for i in range(size)])


def call(kernel, out_shape, args, grid=None, in_specs=None, out_specs=None, scratch=(), flops=0, moved=0):
    kwargs = {}
    if grid is not None:
        kwargs = dict(grid=grid, in_specs=in_specs, out_specs=out_specs)
    return pl.pallas_call(
        kernel,
        out_shape=out_shape,
        scratch_shapes=list(scratch),
        compiler_params=pltpu.CompilerParams(vmem_limit_bytes=VMEM_BYTES),
        cost_estimate=pl.CostEstimate(flops=int(flops), bytes_accessed=int(moved), transcendentals=0),
        **kwargs,
    )(*args)


def struct(*shape, dtype=BF16):
    return jax.ShapeDtypeStruct(shape, dtype)


def hot_rows(count, ids):
    return (lax.broadcasted_iota(I32, (count, ids.shape[1]), 0) == ids).astype(BF16)


def lane_row(block):
    return jnp.concatenate([block[k : k + 1, :] for k in range(block.shape[0])], axis=1)


def received_ids(packet_ref, me, bucket):
    size = packet_ref.shape[0]
    coded = packet_ref[lax.rem(me + bucket, size), PACK:, :].astype(F32)
    half = coded.shape[0] // 2
    return (coded[:half] * float(TILE) + coded[half:]).astype(I32)


def pool_rows(packet_ref):
    size = packet_ref.shape[0]
    return packet_ref[:, :PACK, :].reshape(size * PACK, LANES)


def prepare_kernel(pos_ref, emb_ref, rel_ref, served_ref, ids_ref, embp_ref, relp_ref, packet_ref, wide, coded):
    columns = emb_ref.shape[1]
    pad = embp_ref.shape[0] // 2
    me = pos_ref[0]
    entities = emb_ref.shape[2]
    relation_count = rel_ref.shape[2]
    wide[...] = jnp.zeros_like(wide)
    for half in range(2):
        wide[half * pad : half * pad + columns, :relation_count] = rel_ref[half].astype(F32)
    relp_ref[...] = wide[:, :relation_count].astype(BF16)
    for half in range(2):
        wide[half * pad : half * pad + columns, :] = emb_ref[half].astype(F32)
    embp_ref[...] = wide[...].astype(BF16)
    fetched = jnp.dot(embp_ref[...], hot_rows(entities, served_ref[...]), preferred_element_type=F32)
    fetched = jnp.concatenate([fetched, jnp.zeros((LANES - 2 * pad, fetched.shape[1]), F32)], axis=0)
    size = packet_ref.shape[0]
    packet_ref[:, :PACK, :] = fetched.T.astype(BF16).reshape(size, PACK, LANES)
    buckets, edges = ids_ref.shape
    for bucket in range(buckets):
        block = jnp.concatenate(
            [ids_ref[bucket : bucket + 1, k : k + LANES] for k in range(0, edges, LANES)], axis=0
        )
        high = lax.shift_right_logical(block, 8)
        coded[bucket] = jnp.concatenate([high, block - high * TILE], axis=0).astype(F32).astype(BF16)
    for to in range(size):
        bucket = jnp.minimum(lax.rem(me - to + size, size), buckets - 1)
        packet_ref[to, PACK:, :] = coded[bucket]


def product_kernel(bucket, emb_ref, rel_ref, source_ref, relation_ref, product_ref, rows_ref):
    pad = emb_ref.shape[0] // 2
    source = jnp.dot(
        emb_ref[...], hot_rows(emb_ref.shape[1], source_ref[bucket : bucket + 1, :]), preferred_element_type=F32
    )
    rel = jnp.dot(
        rel_ref[...], hot_rows(rel_ref.shape[1], relation_ref[bucket : bucket + 1, :]), preferred_element_type=F32
    )
    rows_ref[...] = rel.astype(BF16)
    s0, s1, r0, r1 = source[:pad], source[pad:], rel[:pad], rel[pad:]
    product_ref[...] = jnp.concatenate([s0 * r0 - s1 * r1, s0 * r1 + s1 * r0], axis=0).astype(BF16)


def target_kernel(bucket, pos_ref, emb_ref, ids_ref, out_ref):
    if bucket == 0:
        ids = ids_ref[0:1, :]
    else:
        ids = lane_row(received_ids(ids_ref, pos_ref[0], bucket))
    out_ref[...] = jnp.dot(
        emb_ref[...], hot_rows(emb_ref.shape[1], ids), preferred_element_type=F32
    ).astype(BF16)


def score_kernel(pos_ref, packet_ref, *refs):
    buckets = len(refs) - 2
    products, (mine_ref, theirs_ref) = refs[:buckets], refs[buckets:]
    core = pos_ref[1]
    height, edges = products[0].shape
    pool = pool_rows(packet_ref)[:, :height]
    for bucket in range(buckets):
        half, place = divmod(bucket, buckets // 2)
        scores = jnp.dot(pool, products[bucket][...], preferred_element_type=F32)
        spot = slice(place * edges, (place + 1) * edges)

        @pl.when(core == half)
        def _():
            mine_ref[:, spot] = scores

        @pl.when(core != half)
        def _():
            theirs_ref[:, spot] = scores.astype(BF16)


def slope_kernel(pos_ref, own_ref, other_ref, negatives_ref, out_ref):
    core = pos_ref[1]
    count, width = own_ref.shape
    buckets, spans, negs = negatives_ref.shape
    span_len = width // (buckets // 2 * spans)
    for place in range(buckets // 2):
        for span in range(spans):
            drawn = negatives_ref[core * (buckets // 2) + place, span : span + 1, :]
            times = jnp.sum(
                (lax.broadcasted_iota(I32, (count, negs), 0) == drawn).astype(F32), axis=1, keepdims=True
            )
            start = (place * spans + span) * span_len
            spot = slice(start, start + span_len)
            scores = own_ref[:, spot].astype(F32) + other_ref[:, spot].astype(F32)
            out_ref[:, spot] = (times * jax.nn.sigmoid(scores)).astype(BF16)


def bucket_slopes(core, mine_ref, theirs_ref, bucket, buckets, edges):
    half, place = divmod(bucket, buckets // 2)
    spot = slice(place * edges, (place + 1) * edges)
    return jnp.where(core == half, mine_ref[:, spot], theirs_ref[:, spot])


def pool_grad_kernel(pos_ref, mine_ref, theirs_ref, *refs):
    buckets = len(refs) - 1
    out_ref = refs[-1]
    core = pos_ref[1]
    height, edges = refs[0].shape
    total = None
    for bucket in range(buckets):
        slopes = bucket_slopes(core, mine_ref, theirs_ref, bucket, buckets, edges)
        part = lax.dot_general(
            slopes, refs[bucket][...], (((1,), (1,)), ((), ())), preferred_element_type=F32
        )
        total = part if total is None else total + part
    total = jnp.concatenate([total, jnp.zeros((total.shape[0], LANES - height), F32)], axis=1)
    out_ref[...] = total.astype(BF16).reshape(out_ref.shape)


def positive_kernel(*refs):
    out_ref = refs[-1]
    pairs = len(refs) // 2
    rows = []
    for k in range(pairs):
        rows.append(
            jnp.sum(refs[2 * k][...].astype(F32) * refs[2 * k + 1][...].astype(F32), axis=0, keepdims=True)
        )
    rows.append(jnp.zeros((out_ref.shape[0] - pairs, out_ref.shape[1]), F32))
    out_ref[...] = jnp.concatenate(rows, axis=0).astype(BF16)


def final_kernel(buckets, pos_ref, mine_ref, theirs_ref, packet_ref, returned_ref, served_ref, source_ref, target_ref,
                 own_ref, near_ref, far_ref, *refs):
    relation_rows = refs[:buckets]
    targets = refs[buckets : 2 * buckets]
    products = refs[2 * buckets : 3 * buckets]
    out_ref, values, cols = refs[3 * buckets :]
    step = pl.program_id(0)
    height, edges = targets[0].shape
    pad = height // 2
    columns = out_ref.shape[1]
    tiles = out_ref.shape[2] // TILE

    @pl.when(step == 0)
    def _():
        me, core = pos_ref[0], pos_ref[1]
        positive = (
            own_ref[...].astype(F32)
            + near_ref[...].astype(F32)
            + far_ref[0].astype(F32)
            + far_ref[1].astype(F32)
        )
        slope = -jax.nn.sigmoid(-positive)
        pool = pool_rows(packet_ref).astype(F32).T[:height].astype(BF16)
        rows = []
        for bucket in range(buckets):
            slopes = bucket_slopes(core, mine_ref, theirs_ref, bucket, buckets, edges)
            query = jnp.dot(pool, slopes, preferred_element_type=F32)
            total = slope[bucket : bucket + 1] * targets[bucket][...].astype(F32) + query
            rel = relation_rows[bucket][...].astype(F32)
            t0, t1, r0, r1 = total[:pad], total[pad:], rel[:pad], rel[pad:]
            values[:, bucket * edges : (bucket + 1) * edges] = jnp.concatenate(
                [t0 * r0 + t1 * r1, t1 * r0 - t0 * r1], axis=0
            ).astype(BF16)
            rows.append(source_ref[bucket : bucket + 1, :])
        for bucket in range(buckets):
            place = 0 if bucket == 0 else buckets - 1 + bucket
            spot = slice((buckets + bucket) * edges, (buckets + bucket + 1) * edges)
            values[:, spot] = (slope[place : place + 1] * products[bucket][...].astype(F32)).astype(BF16)
            if bucket == 0:
                rows.append(target_ref[0:1, :])
            else:
                rows.append(lane_row(received_ids(packet_ref, me, bucket)))
        back = returned_ref[...].reshape(-1, LANES).astype(F32).T[:height]
        values[:, 2 * buckets * edges :] = back.astype(BF16)
        rows.append(served_ref[...])
        at = 0
        for row in rows:
            for k in range(0, row.shape[1], LANES):
                cols[at : at + LANES, :] = jnp.broadcast_to(row[:, k : k + LANES], (LANES, LANES)).T
                at += LANES

    lane = lax.broadcasted_iota(I32, cols.shape, 1)
    for tile in range(tiles):
        base = (step * tiles + tile) * TILE
        ids = cols[...]
        hot = jnp.concatenate(
            [(ids == lane + (base + k)).astype(BF16) for k in range(0, TILE, LANES)], axis=1
        )
        total = jnp.dot(values[...], hot, preferred_element_type=F32)
        for half in range(2):
            out_ref[half, :, tile * TILE : (tile + 1) * TILE] = total[half * pad : half * pad + columns]


def body(embeddings, relations, source_ids, relation_ids, target_ids, negative_ids, served_rows):
    halves, columns, entities = embeddings.shape
    buckets, edges = source_ids.shape
    relation_count = relations.shape[2]
    size = lax.axis_size("dom")
    pad = -(-columns // 8) * 8
    height = 2 * pad
    pool_count = served_rows.size
    served = served_rows.reshape(1, pool_count)
    position = jnp.stack([lax.axis_index("dom"), lax.axis_index("col") & 1]).astype(I32)
    smem = pl.BlockSpec(memory_space=pltpu.SMEM)
    packet_rows = PACK + 2 * edges // LANES

    def whole(array):
        return pl.BlockSpec(array.shape, lambda *_: (0,) * array.ndim)

    def local(kernel, out, *args, scratch=(), flops=0):
        outs = out if isinstance(out, tuple) else (out,)
        moved = sum(a.size * a.dtype.itemsize for a in args + outs)
        return call(
            kernel,
            out,
            args,
            grid=(1,),
            in_specs=[smem if a is position else whole(a) for a in args],
            out_specs=jax.tree.map(whole, out),
            scratch=scratch,
            flops=flops,
            moved=moved,
        )

    emb, rel, packet = local(
        prepare_kernel,
        (struct(height, entities), struct(height, relation_count), struct(size, packet_rows, LANES)),
        position, embeddings, relations, served, target_ids,
        scratch=(pltpu.VMEM((height, entities), F32), pltpu.VMEM((buckets, packet_rows - PACK, LANES), BF16)),
        flops=2 * LANES * entities * pool_count,
    )
    packet = lax.all_to_all(packet, "dom", split_axis=0, concat_axis=0, tiled=True)
    products, relation_rows = [], []
    for bucket in range(buckets):
        product, rows = local(
            functools.partial(product_kernel, bucket),
            (struct(height, edges), struct(height, edges)),
            emb, rel, source_ids, relation_ids,
            flops=2 * LANES * (entities + relation_count) * edges,
        )
        products.append(product)
        relation_rows.append(rows)
    owned_targets = []
    for bucket in range(buckets):
        owned_targets.append(
            local(
                functools.partial(target_kernel, bucket),
                struct(height, edges),
                position, emb, target_ids if bucket == 0 else packet,
                flops=2 * LANES * entities * edges,
            )
        )
    targets = [owned_targets[0]] + [rotate(owned_targets[b], "dom", b) for b in range(1, buckets)]
    owned_products = [products[0]] + [rotate(products[b], "dom", -b) for b in range(1, buckets)]

    width = buckets // 2 * edges
    mine, theirs = local(
        score_kernel,
        (struct(pool_count, width, dtype=F32), struct(pool_count, width)),
        position, packet, *products,
        flops=2 * LANES * pool_count * edges * buckets,
    )
    pair = (mine + swap(theirs, "col", 1).astype(F32)).astype(BF16)
    slopes_mine = local(
        slope_kernel, struct(pool_count, width), position, pair, swap(pair, "col", 2), negative_ids,
    )
    slopes_theirs = swap(slopes_mine, "col", 1)
    pool_grad = local(
        pool_grad_kernel, struct(size, PACK, LANES), position, slopes_mine, slopes_theirs, *products,
        flops=2 * LANES * pool_count * edges * buckets,
    )
    returned = lax.all_to_all(pool_grad, "dom", split_axis=0, concat_axis=0, tiled=True)

    pairs = [products[0], owned_targets[0]]
    for b in range(1, buckets):
        pairs += [products[b], targets[b]]
    for b in range(1, buckets):
        pairs += [owned_products[b], owned_targets[b]]
    own = local(positive_kernel, struct(16, edges), *pairs)
    near = swap(own, "col", 1)
    far = swap(jnp.stack([own, near]), "col", 2)

    args = [position, slopes_mine, slopes_theirs, packet, returned, served, source_ids, target_ids, own, near, far]
    args += relation_rows + targets + owned_products
    total = 2 * buckets * edges + pool_count
    steps = 4
    return call(
        functools.partial(final_kernel, buckets),
        struct(halves, columns, entities, dtype=F32),
        args,
        grid=(steps,),
        in_specs=[smem if a is position else whole(a) for a in args],
        out_specs=pl.BlockSpec((halves, columns, entities // steps), lambda i: (0, 0, i)),
        scratch=(pltpu.VMEM((height, total), BF16), pltpu.VMEM((total, LANES), I32)),
        flops=2 * LANES * total * entities,
        moved=sum(a.size * a.dtype.itemsize for a in args) + 4 * halves * columns * entities,
    )


def solution(mesh):
    placed = (
        P(None, "col", "dom"),
        P(None, "col", None),
        P(None, "dom"),
        P(None, "dom"),
        P(None, "dom"),
        P(None, "dom", None),
        P("dom", None),
    )
    return jax.shard_map(
        body, mesh=mesh, in_specs=placed, out_specs=P(None, "col", "dom"), check_vma=False
    )
```

```python
import functools

import jax
import jax.numpy as jnp
from jax import lax
from jax.experimental import pallas as pl
from jax.experimental.pallas import tpu as pltpu
from jax.sharding import PartitionSpec as P

BF16 = jnp.bfloat16
F32 = jnp.float32
I32 = jnp.int32
LANES = 128
PACK = 16
TILE = 256
VMEM_BASE = 9 << 20
VMEM_PER_POOL_ROW = 24 << 10


def rotate(shard, axis, by):
    size = lax.axis_size(axis)
    return lax.ppermute(shard, axis, [(i, (i + by) % size) for i in range(size)])


def swap(shard, axis, bit):
    size = lax.axis_size(axis)
    return lax.ppermute(shard, axis, [(i, i ^ bit) for i in range(size)])


def exchange(first, rest, axis):
    size = 2 * first.shape[0]
    half = size // 2
    parts, origins = (first[None], swap(rest, axis, half)[None]), [0, half]
    while half > 1:
        held = jnp.concatenate(parts, axis=0)
        half //= 2
        parts = (held[:, :half], swap(held[:, half:], axis, half))
        origins = origins + [origin ^ half for origin in origins]
    return parts, tuple(origins)


def struct(*shape, dtype=BF16):
    return jax.ShapeDtypeStruct(shape, dtype)


def hot_rows(count, ids):
    return (lax.broadcasted_iota(I32, (count, ids.shape[1]), 0) == ids).astype(BF16)


def lane_row(block):
    return jnp.concatenate([block[k : k + 1, :] for k in range(block.shape[0])], axis=1)


def lines(array):
    halves, columns, count = array.shape
    cut = array.reshape(halves, columns, count // LANES, LANES)
    return cut.transpose(1, 2, 0, 3).reshape(-1, LANES)


def from_lines(array, halves, columns, count):
    cut = array.reshape(columns, count // LANES, halves, LANES)
    return cut.transpose(2, 0, 1, 3).reshape(halves, columns, count)


def unpack_lines(lines_ref, wide, out_ref):
    pad = out_ref.shape[0] // 2
    chunks = out_ref.shape[1] // LANES
    rows = lines_ref.shape[0]
    columns = rows // (2 * chunks)
    wide[:rows, :] = lines_ref[...].astype(F32)
    for k in range(chunks):
        parts = []
        for half in range(2):
            parts.append(wide[pl.ds(2 * k + half, columns, stride=2 * chunks), :])
            parts.append(jnp.zeros((pad - columns, LANES), F32))
        out_ref[:, k * LANES : (k + 1) * LANES] = jnp.concatenate(parts, axis=0).astype(BF16)


def prepare_kernel(targets_at, pos_ref, ids_ref, served_ref, emb_ref, embp_ref, packet_ref, row_ref, wide, coded):
    height = embp_ref.shape[0]
    me = pos_ref[0]
    edges = ids_ref.shape[1]
    buckets = coded.shape[0]
    for bucket in range(buckets):
        row = targets_at + bucket
        block = jnp.concatenate([ids_ref[row : row + 1, k : k + LANES] for k in range(0, edges, LANES)], axis=0)
        high = lax.shift_right_logical(block, 8)
        coded[bucket] = jnp.concatenate([high, block - high * TILE], axis=0).astype(F32).astype(BF16)
    size = packet_ref.shape[0]
    row_ref[...] = jnp.concatenate([served_ref[k : k + 1, :] for k in range(size)], axis=1)
    unpack_lines(emb_ref, wide, embp_ref)
    fetched = jnp.dot(embp_ref[...], hot_rows(embp_ref.shape[1], row_ref[...]), preferred_element_type=F32)
    fetched = jnp.concatenate([fetched, jnp.zeros((LANES - height, fetched.shape[1]), F32)], axis=0)
    packet_ref[:, :PACK, :] = fetched.T.astype(BF16).reshape(size, PACK, LANES)
    for to in range(size):
        bucket = jnp.minimum(lax.rem(me - to + size, size), buckets - 1)
        packet_ref[to, PACK:, :] = coded[bucket]


def settle_kernel(targets_at, pos_ref, ids_ref, packet_ref, pool_ref, asked_ref):
    me = pos_ref[0]
    size = packet_ref.shape[0]
    pool_ref[...] = packet_ref[:, :PACK, :].reshape(pool_ref.shape)
    asked_ref[0:1, :] = ids_ref[targets_at : targets_at + 1, :]
    for bucket in range(1, asked_ref.shape[0]):
        coded = packet_ref[lax.rem(me + bucket, size), PACK:, :].astype(F32)
        half = coded.shape[0] // 2
        asked_ref[bucket : bucket + 1, :] = lane_row((coded[:half] * float(TILE) + coded[half:]).astype(I32))


def relation_kernel(rel_ref, relp_ref, wide):
    unpack_lines(rel_ref, wide, relp_ref)


def take(rows_ref, ids):
    return jnp.dot(rows_ref[...], hot_rows(rows_ref.shape[1], ids), preferred_element_type=F32)


def make_product(emb_ref, rel_ref, ids_ref, buckets, bucket, product_ref, rows_ref):
    pad = emb_ref.shape[0] // 2
    source = take(emb_ref, ids_ref[bucket : bucket + 1, :])
    rel = take(rel_ref, ids_ref[buckets + bucket : buckets + bucket + 1, :])
    rows_ref[...] = rel.astype(BF16)
    s0, s1, r0, r1 = source[:pad], source[pad:], rel[:pad], rel[pad:]
    product_ref[...] = jnp.concatenate([s0 * r0 - s1 * r1, s0 * r1 + s1 * r0], axis=0).astype(BF16)


def product_kernel(emb_ref, rel_ref, ids_ref, *outs):
    buckets = len(outs) // 2
    for bucket in list(range(1, buckets)) + [0]:
        make_product(emb_ref, rel_ref, ids_ref, buckets, bucket, outs[bucket], outs[buckets + bucket])


def target_kernel(chosen, emb_ref, asked_ref, *refs):
    for bucket, out_ref in zip(chosen, refs[-len(chosen) :]):
        out_ref[...] = take(emb_ref, asked_ref[bucket : bucket + 1, :]).astype(BF16)


def pair_kernel(mine_ref, *refs):
    count = len(refs) // 2
    width = refs[0].shape[1]
    for k in range(count):
        spot = slice(k * width, (k + 1) * width)
        refs[count + k][...] = (mine_ref[:, spot] + refs[k][...].astype(F32)).astype(BF16)


def score_kernel(buckets, pos_ref, pool_ref, *refs):
    products, mine_ref, pieces = refs[:buckets], refs[buckets], refs[buckets + 1 :]
    core = pos_ref[1]
    height, edges = products[0].shape
    per = len(pieces) // (buckets // 2)
    cut = edges // per
    pool = pool_ref[:, :height]
    for bucket in range(buckets):
        half, place = divmod(bucket, buckets // 2)
        scores = jnp.dot(pool, products[bucket][...], preferred_element_type=F32)

        @pl.when(core == half)
        def _():
            mine_ref[:, place * edges : (place + 1) * edges] = scores

        @pl.when(core != half)
        def _():
            for k in range(per):
                pieces[place * per + k][...] = scores[:, k * cut : (k + 1) * cut].astype(BF16)


def slope_kernel(pieces, pos_ref, negatives_ref, *refs):
    out_ref = refs[-1]
    core = pos_ref[1]
    count, width = refs[0].shape
    buckets, spans, negs = negatives_ref.shape
    span_len = width * pieces // (buckets // 2 * spans)
    for place in range(buckets // 2):
        for span in range(spans):
            drawn = negatives_ref[core * (buckets // 2) + place, span : span + 1, :]
            times = jnp.sum(
                (lax.broadcasted_iota(I32, (count, negs), 0) == drawn).astype(F32), axis=1, keepdims=True
            )
            start = (place * spans + span) * span_len
            piece, offset = divmod(start, width)
            spot = slice(offset, offset + span_len)
            scores = refs[piece][:, spot].astype(F32) + refs[pieces + piece][:, spot].astype(F32)
            out_ref[:, start : start + span_len] = (times * jax.nn.sigmoid(scores)).astype(BF16)


def bucket_slopes(core, mine_ref, theirs_ref, bucket, buckets, edges):
    half, place = divmod(bucket, buckets // 2)
    spot = slice(place * edges, (place + 1) * edges)
    return jnp.where(core == half, mine_ref[:, spot], theirs_ref[:, spot])


def pool_grad_kernel(buckets, groups, ring, pos_ref, mine_ref, theirs_ref, pool_ref, *refs):
    held, query_ref = refs[-1], refs[-2]
    outs = refs[-2 - len(groups) : -2]
    core = pos_ref[1]
    height, edges = refs[0].shape
    pool = pool_ref[...].astype(F32).T[:height].astype(BF16)
    total = None
    for bucket in range(buckets):
        slopes = bucket_slopes(core, mine_ref, theirs_ref, bucket, buckets, edges)
        query_ref[:, bucket * edges : (bucket + 1) * edges] = jnp.dot(pool, slopes, preferred_element_type=F32)
        part = lax.dot_general(
            slopes, refs[bucket][...], (((1,), (1,)), ((), ())), preferred_element_type=F32
        )
        total = part if total is None else total + part
    total = jnp.concatenate([total, jnp.zeros((total.shape[0], LANES - height), F32)], axis=1)
    held[...] = total.astype(BF16).reshape(held.shape)
    me = pos_ref[0]
    size = held.shape[0]
    for group, out_ref in zip(groups, outs):
        for k, offset in enumerate(group):
            out_ref[k] = held[lax.rem(me + offset, size) if ring else me ^ offset]


def positive_kernel(*refs):
    out_ref = refs[-1]
    pairs = len(refs) // 2
    rows = []
    for k in range(pairs):
        rows.append(
            jnp.sum(refs[2 * k][...].astype(F32) * refs[2 * k + 1][...].astype(F32), axis=0, keepdims=True)
        )
    rows.append(jnp.zeros((out_ref.shape[0] - pairs, out_ref.shape[1]), F32))
    out_ref[...] = jnp.concatenate(rows, axis=0).astype(BF16)


def scale_kernel(buckets, columns, own_ref, near_ref, far_ref, *refs):
    positive = (
        own_ref[...].astype(F32) + near_ref[...].astype(F32) + far_ref[0].astype(F32) + far_ref[1].astype(F32)
    )
    slope = -jax.nn.sigmoid(-positive)
    last = buckets - 1
    targets, product, riders = refs[:buckets], refs[buckets], refs[buckets + 1 : -buckets - 2]
    slope_ref, outs = refs[-buckets - 2], refs[-buckets - 1 :]
    slope_ref[...] = slope
    for bucket in range(buckets):
        outs[bucket][...] = (slope[bucket : bucket + 1] * targets[bucket][...].astype(F32)).astype(BF16)
    outs[buckets][...] = (slope[last : last + 1] * product[...].astype(F32)).astype(BF16)
    for k, out_ref in enumerate(outs[1:last] + outs[buckets:]):
        if riders:
            value = out_ref[...].astype(F32)
            rows = [value[:columns]]
            for rider in riders:
                block = rider[k].astype(F32)
                rows += [lane_row(block[k : k + 8]) for k in range(0, PACK, 8)]
            rows.append(value[columns + 2 * len(riders) :])
            out_ref[...] = jnp.concatenate(rows, axis=0).astype(BF16)


def rider_blocks(pull_ref, columns, count):
    rows = pull_ref[...].astype(F32)[columns : columns + 2 * count]
    blocks = []
    for at in range(count):
        lines_of = [
            rows[2 * at + part : 2 * at + part + 1, k * LANES : (k + 1) * LANES] for part in range(2) for k in range(8)
        ]
        blocks.append(jnp.concatenate(lines_of, axis=0).astype(BF16))
    return blocks


def source_values(total, relation_ref):
    rel = relation_ref[...].astype(F32)
    pad = rel.shape[0] // 2
    t0, t1, r0, r1 = total[:pad], total[pad:], rel[:pad], rel[pad:]
    return jnp.concatenate([t0 * r0 + t1 * r1, t1 * r0 - t0 * r1], axis=0).astype(BF16)


def write_columns(cols, rows):
    at = 0
    for row in rows:
        for k in range(0, row.shape[1], LANES):
            cols[at : at + LANES, :] = jnp.broadcast_to(row[:, k : k + LANES], (LANES, LANES)).T
            at += LANES


def scattered(values, cols, base):
    lane = lax.broadcasted_iota(I32, cols.shape, 1)
    ids = cols[...]
    hot = jnp.concatenate([(ids == lane + (base + k)).astype(BF16) for k in range(0, TILE, LANES)], axis=1)
    return jnp.dot(values[...], hot, preferred_element_type=F32)


def fill(values, cols, columns_of, rows):
    at = 0
    for value in columns_of:
        values[:, at : at + value.shape[1]] = value
        at += value.shape[1]
    write_columns(cols, rows)


def scatter_all(out_ref, values, cols, held_ref=None):
    for tile in range(out_ref.shape[1] // TILE):
        spot = slice(tile * TILE, (tile + 1) * TILE)
        total = scattered(values, cols, tile * TILE)
        out_ref[:, spot] = total if held_ref is None else total + held_ref[:, spot]


def home_kernel(ids_ref, asked_ref, slope_ref, query_ref, *refs):
    out_ref, values, cols = refs[-3:]
    buckets, edges = asked_ref.shape
    last = buckets - 1
    products, pulls, relation_rows = refs[:last], refs[last : last + 2], refs[last + 2 : last + 4]
    columns_of = [
        (slope_ref[bucket : bucket + 1] * products[bucket][...].astype(F32)).astype(BF16) for bucket in range(last)
    ]
    rows = [asked_ref[bucket : bucket + 1, :] for bucket in range(last)]
    for bucket, pull, rel in zip((0, last), pulls, relation_rows):
        query = query_ref[:, bucket * edges : (bucket + 1) * edges]
        columns_of.append(source_values(pull[...].astype(F32) + query, rel))
        rows.append(ids_ref[bucket : bucket + 1, :])
    fill(values, cols, columns_of, rows)
    scatter_all(out_ref, values, cols)


def middle_kernel(ids_ref, query_ref, *refs):
    held_ref, out_ref, values, cols = refs[-4:]
    count = (len(refs) - 4) // 2
    relation_rows, pulls = refs[:count], refs[count : 2 * count]
    edges = pulls[0].shape[1]
    columns_of, rows = [], []
    for k in range(count):
        query = query_ref[:, (k + 1) * edges : (k + 2) * edges]
        columns_of.append(source_values(pulls[k][...].astype(F32) + query, relation_rows[k]))
        rows.append(ids_ref[k + 1 : k + 2, :])
    fill(values, cols, columns_of, rows)
    scatter_all(out_ref, values, cols, held_ref)


def final_kernel(plan, origins, pos_ref, asked_ref, served_ref, push_ref, *refs):
    held_ref, out_ref, values, cols, back = refs[-5:]
    buckets, edges = asked_ref.shape
    others = refs[:-5]
    step = pl.program_id(0)
    height = push_ref.shape[0]
    pad = height // 2
    columns, lines_here, _ = out_ref.shape
    flat = out_ref.reshape(columns * lines_here, LANES)

    @pl.when(step == 0)
    def _():
        me = pos_ref[0]
        size = back.shape[0]
        if plan is not None:
            carriers, hop, left = plan
            pulls, home, direct = others[: len(carriers) - 1], others[len(carriers) - 1], others[len(carriers) :]
            back[me] = home[0]
            for carrier, ref in zip(carriers, (*pulls, push_ref)):
                for block, way in zip(rider_blocks(ref, columns, 2), (carrier, carrier + hop)):
                    back[lax.rem(me + 2 * size - way, size)] = block
            for way, ref in zip(left, direct):
                back[lax.rem(me + size - way, size)] = ref[0]
        else:
            blocks = [part[k, 0] for part in others for k in range(part.shape[0])]
            for origin, block in zip(origins, blocks):
                back[me ^ origin] = block
        returned = back[...].reshape(-1, LANES).astype(F32).T[:height].astype(BF16)
        fill(values, cols, [push_ref[...], returned], [asked_ref[buckets - 1 : buckets, :], served_ref[...]])

    tiles = lines_here * LANES // (2 * TILE)
    for tile in range(tiles):
        spot = slice(tile * TILE, (tile + 1) * TILE)
        total = scattered(values, cols, (step * tiles + tile) * TILE) + held_ref[:, spot]
        for k in range(TILE // LANES):
            for half in range(2):
                row = 2 * (tile * (TILE // LANES) + k) + half
                flat[pl.ds(row, columns, stride=lines_here), :] = total[
                    half * pad : half * pad + columns, k * LANES : (k + 1) * LANES
                ]


def body(embeddings, relations, source_ids, relation_ids, target_ids, negative_ids, served_rows):
    halves, columns, entities = embeddings.shape
    buckets, edges = source_ids.shape
    relation_count = relations.shape[2]
    size = lax.axis_size("dom")
    height = -(-columns // 8) * 16
    pool_count = served_rows.size
    position = jnp.stack([lax.axis_index("dom"), lax.axis_index("col") & 1]).astype(I32)
    smem = pl.BlockSpec(memory_space=pltpu.SMEM)
    vmem = pl.BlockSpec(memory_space=pltpu.VMEM)
    anywhere = pl.BlockSpec(memory_space=pl.ANY)
    packet_rows = PACK + 2 * edges // LANES
    limit = VMEM_BASE + pool_count * VMEM_PER_POOL_ROW

    def local(kernel, out, *args, scratch=(), flops=0, grid=None, out_specs=None, specs=None):
        outs = out if isinstance(out, tuple) else (out,)
        chosen = [smem if a is position else vmem for a in args]
        for place, spec in (specs or {}).items():
            chosen[place] = spec
        extra = {} if grid is None else {"grid": grid}
        return pl.pallas_call(
            kernel,
            out_shape=out,
            in_specs=chosen,
            out_specs=jax.tree.map(lambda _: vmem, out) if out_specs is None else out_specs,
            scratch_shapes=list(scratch),
            compiler_params=pltpu.CompilerParams(vmem_limit_bytes=limit),
            cost_estimate=pl.CostEstimate(
                flops=int(flops),
                bytes_accessed=int(sum(a.size * a.dtype.itemsize for a in args + outs)),
                transcendentals=0,
            ),
            **extra,
        )(*args)

    edge_rows = struct(height, edges)
    gather_flops = 2 * LANES * entities * edges
    ids = jnp.concatenate([source_ids, relation_ids, target_ids], axis=0)
    emb_lines, rel_lines = lines(embeddings), lines(relations)
    emb, packet, served = local(
        functools.partial(prepare_kernel, 2 * buckets),
        (struct(height, entities), struct(size, packet_rows, LANES), struct(1, pool_count, dtype=I32)),
        position, ids, served_rows, emb_lines,
        scratch=(
            pltpu.VMEM(emb_lines.shape, F32),
            pltpu.VMEM((buckets, packet_rows - PACK, LANES), BF16),
        ),
        flops=2 * LANES * entities * pool_count,
    )
    packet = lax.all_to_all(packet, "dom", split_axis=0, concat_axis=0, tiled=True)
    pool, asked = local(
        functools.partial(settle_kernel, 2 * buckets),
        (struct(pool_count, LANES), struct(buckets, edges, dtype=I32)),
        position, ids, packet,
    )
    rel = local(
        relation_kernel, struct(height, relation_count), rel_lines, scratch=(pltpu.VMEM(rel_lines.shape, F32),)
    )
    made = local(product_kernel, (edge_rows,) * (2 * buckets), emb, rel, ids, flops=gather_flops * buckets)
    products, relation_rows = made[:buckets], made[buckets:]
    last = buckets - 1

    def take_targets(chosen, *after):
        return local(
            functools.partial(target_kernel, chosen), (edge_rows,) * len(chosen), emb, asked, *after,
            specs={2 + k: anywhere for k in range(len(after))},
            flops=gather_flops * len(chosen),
        )

    owned_products = [products[0]] + [rotate(products[b], "dom", -b) for b in range(1, last)]
    (last_target,) = take_targets((last,))
    last_target = rotate(last_target, "dom", last)
    width = buckets // 2 * edges
    pieces = 4
    piece = struct(pool_count, width // pieces)
    mine, *theirs = local(
        functools.partial(score_kernel, buckets),
        (struct(pool_count, width, dtype=F32),) + (piece,) * pieces,
        position, pool, *products,
        flops=2 * LANES * pool_count * edges * buckets,
    )
    pair = local(pair_kernel, (piece,) * pieces, mine, *[swap(part, "col", 1) for part in theirs])
    targets = [*take_targets(tuple(range(last))), last_target]
    after = [targets[0], *owned_products[1:], last_target]
    slopes_mine = local(
        functools.partial(slope_kernel, pieces), struct(pool_count, width),
        position, negative_ids, *pair, *[swap(part, "col", 2) for part in pair], *after,
        specs={2 + 2 * pieces + k: anywhere for k in range(len(after))},
    )
    slopes_theirs = swap(slopes_mine, "col", 1)
    pairs = [x for b in range(last) for x in (owned_products[b], targets[b])] + [products[last], last_target]
    own = local(positive_kernel, struct(PACK, edges), *pairs)
    near = swap(own, "col", 1)
    far = swap(jnp.stack([own, near]), "col", 2)
    plan = None
    groups = [list(range(size // 2)), list(range(size // 2, size))]
    if size == 2 * buckets and columns + 4 <= height // 2:
        carriers = [*range(1, last), size - last]

        def left_of(hop):
            return sorted(set(range(1, size)) - set(carriers) - {(hop + c) % size for c in carriers})

        hop = min(range(1, size), key=lambda h: len(left_of(h)))
        plan = (tuple(carriers), hop, tuple(left_of(hop)))
        groups = [[0], carriers, [hop + c for c in carriers]] + [[way] for way in left_of(hop)]
    *sent, query = local(
        functools.partial(pool_grad_kernel, buckets, groups, plan is not None),
        tuple(struct(len(group), PACK, LANES) for group in groups)
        + (struct(height, buckets * edges, dtype=F32),),
        position, slopes_mine, slopes_theirs, pool, *products,
        scratch=(pltpu.VMEM((size, PACK, LANES), BF16),),
        flops=4 * LANES * pool_count * edges * buckets,
    )
    if plan is None:
        riders, origins = (), None
        parts, origins = exchange(*sent, "dom")
    else:
        riders, origins = (sent[1], rotate(sent[2], "dom", hop)), None
        direct = [rotate(block, "dom", way) for way, block in zip(plan[2], sent[3:])]
    slope, *scaled = local(
        functools.partial(scale_kernel, buckets, columns),
        (struct(PACK, edges, dtype=F32),) + (edge_rows,) * (buckets + 1),
        own, near, far, *targets, products[last], *riders,
    )
    pulls = [rotate(scaled[b], "dom", b) for b in range(1, last)]
    push = rotate(scaled[buckets], "dom", -last)
    if plan is not None:
        parts = (*pulls, sent[0], *direct)
    count = (buckets + 1) * edges
    held = local(
        home_kernel,
        struct(height, entities, dtype=F32),
        ids, asked, slope, query, *owned_products, scaled[0], scaled[last], relation_rows[0], relation_rows[last],
        scratch=(pltpu.VMEM((height, count), BF16), pltpu.VMEM((count, LANES), I32)),
    )
    count = (last - 1) * edges
    held = local(
        middle_kernel,
        struct(height, entities, dtype=F32),
        ids, query, *relation_rows[1:last], *pulls, held,
        scratch=(pltpu.VMEM((height, count), BF16), pltpu.VMEM((count, LANES), I32)),
        flops=2 * LANES * count * entities,
    )
    steps = 4
    count = edges + pool_count
    args = [position, asked, served, push, *parts, held]
    grad = local(
        functools.partial(final_kernel, plan, origins),
        struct(columns, 2 * entities // LANES, LANES, dtype=F32),
        *args,
        grid=(steps,),
        specs={len(args) - 1: pl.BlockSpec((height, entities // steps), lambda i: (0, i))},
        out_specs=pl.BlockSpec((columns, 2 * entities // LANES // steps, LANES), lambda i: (0, i, 0)),
        scratch=(
            pltpu.VMEM((height, count), BF16),
            pltpu.VMEM((count, LANES), I32),
            pltpu.VMEM((size, PACK, LANES), BF16),
        ),
        flops=2 * LANES * count * entities,
    )
    return from_lines(grad, halves, columns, entities)


def solution(mesh):
    placed = (
        P(None, "col", "dom"),
        P(None, "col", None),
        P(None, "dom"),
        P(None, "dom"),
        P(None, "dom"),
        P(None, "dom", None),
        P("dom", None),
    )
    return jax.shard_map(
        body, mesh=mesh, in_specs=placed, out_specs=P(None, "col", "dom"), check_vma=False
    )
```

```python
import functools

import jax
import jax.numpy as jnp
from jax import lax
from jax.experimental import pallas as pl
from jax.experimental.pallas import tpu as pltpu
from jax.sharding import PartitionSpec as P

BF16 = jnp.bfloat16
F32 = jnp.float32
I32 = jnp.int32
LANES = 128
PACK = 16
TILE = 256
VMEM_BASE = 9 << 20
VMEM_PER_POOL_ROW = 24 << 10


def rotate(shard, axis, by):
    size = lax.axis_size(axis)
    return lax.ppermute(shard, axis, [(i, (i + by) % size) for i in range(size)])


def swap(shard, axis, bit):
    size = lax.axis_size(axis)
    return lax.ppermute(shard, axis, [(i, i ^ bit) for i in range(size)])


def exchange(first, rest, axis):
    size = 2 * first.shape[0]
    half = size // 2
    parts, origins = (first[None], swap(rest, axis, half)[None]), [0, half]
    while half > 1:
        held = jnp.concatenate(parts, axis=0)
        half //= 2
        parts = (held[:, :half], swap(held[:, half:], axis, half))
        origins = origins + [origin ^ half for origin in origins]
    return parts, tuple(origins)


def struct(*shape, dtype=BF16):
    return jax.ShapeDtypeStruct(shape, dtype)


def hot_rows(count, ids):
    return (lax.broadcasted_iota(I32, (count, ids.shape[1]), 0) == ids).astype(BF16)


def lane_row(block):
    return jnp.concatenate([block[k : k + 1, :] for k in range(block.shape[0])], axis=1)


def lines(array):
    halves, columns, count = array.shape
    cut = array.reshape(halves, columns, count // LANES, LANES)
    return cut.transpose(1, 2, 0, 3).reshape(-1, LANES)


def from_lines(array, halves, columns, count):
    cut = array.reshape(columns, count // LANES, halves, LANES)
    return cut.transpose(2, 0, 1, 3).reshape(halves, columns, count)


def unpack_lines(lines_ref, wide, out_ref):
    pad = out_ref.shape[0] // 2
    chunks = out_ref.shape[1] // LANES
    rows = lines_ref.shape[0]
    columns = rows // (2 * chunks)
    wide[:rows, :] = lines_ref[...].astype(F32)
    for k in range(chunks):
        parts = []
        for half in range(2):
            parts.append(wide[pl.ds(2 * k + half, columns, stride=2 * chunks), :])
            parts.append(jnp.zeros((pad - columns, LANES), F32))
        out_ref[:, k * LANES : (k + 1) * LANES] = jnp.concatenate(parts, axis=0).astype(BF16)


def prepare_kernel(buckets, cap, pos_ref, ids_ref, emb_ref, after_ref, embp_ref, packet_ref, row_ref, wide, coded):
    height = embp_ref.shape[0]
    me = pos_ref[0]
    edges = ids_ref.shape[1]
    for bucket in range(buckets):
        row = 2 * buckets + bucket
        block = jnp.concatenate([ids_ref[row : row + 1, k : k + LANES] for k in range(0, edges, LANES)], axis=0)
        high = lax.shift_right_logical(block, 8)
        coded[bucket] = jnp.concatenate([high, block - high * TILE], axis=0).astype(F32).astype(BF16)
    size = packet_ref.shape[0]
    row_ref[...] = jnp.concatenate(
        [ids_ref[3 * buckets + k : 3 * buckets + k + 1, :cap] for k in range(size)], axis=1
    )
    unpack_lines(emb_ref, wide, embp_ref)
    fetched = jnp.dot(embp_ref[...], hot_rows(embp_ref.shape[1], row_ref[...]), preferred_element_type=F32)
    fetched = jnp.concatenate([fetched, jnp.zeros((LANES - height, fetched.shape[1]), F32)], axis=0)
    packet_ref[:, :PACK, :] = fetched.T.astype(BF16).reshape(size, PACK, LANES)
    for to in range(size):
        bucket = jnp.minimum(lax.rem(me - to + size, size), buckets - 1)
        packet_ref[to, PACK:, :] = coded[bucket]


def settle_kernel(targets_at, pos_ref, ids_ref, packet_ref, pool_ref, asked_ref):
    me = pos_ref[0]
    size = packet_ref.shape[0]
    pool_ref[...] = packet_ref[:, :PACK, :].reshape(pool_ref.shape)
    asked_ref[0:1, :] = ids_ref[targets_at : targets_at + 1, :]
    for bucket in range(1, asked_ref.shape[0]):
        coded = packet_ref[lax.rem(me + bucket, size), PACK:, :].astype(F32)
        half = coded.shape[0] // 2
        asked_ref[bucket : bucket + 1, :] = lane_row((coded[:half] * float(TILE) + coded[half:]).astype(I32))


def relation_kernel(rel_ref, relp_ref, wide):
    unpack_lines(rel_ref, wide, relp_ref)


def take(rows_ref, ids):
    return jnp.dot(rows_ref[...], hot_rows(rows_ref.shape[1], ids), preferred_element_type=F32)


def make_product(emb_ref, rel_ref, ids_ref, buckets, bucket, product_ref, rows_ref):
    pad = emb_ref.shape[0] // 2
    source = take(emb_ref, ids_ref[bucket : bucket + 1, :])
    rel = take(rel_ref, ids_ref[buckets + bucket : buckets + bucket + 1, :])
    rows_ref[...] = rel.astype(BF16)
    s0, s1, r0, r1 = source[:pad], source[pad:], rel[:pad], rel[pad:]
    product_ref[...] = jnp.concatenate([s0 * r0 - s1 * r1, s0 * r1 + s1 * r0], axis=0).astype(BF16)


def product_kernel(emb_ref, rel_ref, ids_ref, *outs):
    buckets = len(outs) // 2
    for bucket in list(range(1, buckets)) + [0]:
        make_product(emb_ref, rel_ref, ids_ref, buckets, bucket, outs[bucket], outs[buckets + bucket])


def target_kernel(chosen, emb_ref, asked_ref, *refs):
    for bucket, out_ref in zip(chosen, refs[-len(chosen) :]):
        out_ref[...] = take(emb_ref, asked_ref[bucket : bucket + 1, :]).astype(BF16)


def pair_kernel(mine_ref, *refs):
    count = len(refs) // 2
    width = refs[0].shape[1]
    for k in range(count):
        spot = slice(k * width, (k + 1) * width)
        refs[count + k][...] = (mine_ref[:, spot] + refs[k][...].astype(F32)).astype(BF16)


def score_kernel(buckets, pos_ref, pool_ref, *refs):
    products, mine_ref, pieces = refs[:buckets], refs[buckets], refs[buckets + 1 :]
    core = pos_ref[1]
    height, edges = products[0].shape
    per = len(pieces) // (buckets // 2)
    cut = edges // per
    pool = pool_ref[:, :height]
    for bucket in range(buckets):
        half, place = divmod(bucket, buckets // 2)
        scores = jnp.dot(pool, products[bucket][...], preferred_element_type=F32)

        @pl.when(core == half)
        def _():
            mine_ref[:, place * edges : (place + 1) * edges] = scores

        @pl.when(core != half)
        def _():
            for k in range(per):
                pieces[place * per + k][...] = scores[:, k * cut : (k + 1) * cut].astype(BF16)


def slope_kernel(pieces, pos_ref, negatives_ref, *refs):
    out_ref = refs[-1]
    core = pos_ref[1]
    count, width = refs[0].shape
    buckets, spans, negs = negatives_ref.shape
    span_len = width * pieces // (buckets // 2 * spans)
    for place in range(buckets // 2):
        for span in range(spans):
            drawn = negatives_ref[core * (buckets // 2) + place, span : span + 1, :]
            times = jnp.sum(
                (lax.broadcasted_iota(I32, (count, negs), 0) == drawn).astype(F32), axis=1, keepdims=True
            )
            start = (place * spans + span) * span_len
            piece, offset = divmod(start, width)
            spot = slice(offset, offset + span_len)
            scores = refs[piece][:, spot].astype(F32) + refs[pieces + piece][:, spot].astype(F32)
            out_ref[:, start : start + span_len] = (times * jax.nn.sigmoid(scores)).astype(BF16)


def bucket_slopes(core, mine_ref, theirs_ref, bucket, buckets, edges):
    half, place = divmod(bucket, buckets // 2)
    spot = slice(place * edges, (place + 1) * edges)
    return jnp.where(core == half, mine_ref[:, spot], theirs_ref[:, spot])


def pool_grad_kernel(buckets, groups, ring, pos_ref, mine_ref, theirs_ref, pool_ref, *refs):
    held, query_ref = refs[-1], refs[-2]
    outs = refs[-2 - len(groups) : -2]
    core = pos_ref[1]
    height, edges = refs[0].shape
    pool = pool_ref[...].astype(F32).T[:height].astype(BF16)
    total = None
    for bucket in range(buckets):
        slopes = bucket_slopes(core, mine_ref, theirs_ref, bucket, buckets, edges)
        query_ref[:, bucket * edges : (bucket + 1) * edges] = jnp.dot(pool, slopes, preferred_element_type=F32)
        part = lax.dot_general(
            slopes, refs[bucket][...], (((1,), (1,)), ((), ())), preferred_element_type=F32
        )
        total = part if total is None else total + part
    total = jnp.concatenate([total, jnp.zeros((total.shape[0], LANES - height), F32)], axis=1)
    held[...] = total.astype(BF16).reshape(held.shape)
    me = pos_ref[0]
    size = held.shape[0]
    for group, out_ref in zip(groups, outs):
        for k, offset in enumerate(group):
            out_ref[k] = held[lax.rem(me + offset, size) if ring else me ^ offset]


def positive_kernel(*refs):
    out_ref = refs[-1]
    pairs = len(refs) // 2
    rows = []
    for k in range(pairs):
        rows.append(
            jnp.sum(refs[2 * k][...].astype(F32) * refs[2 * k + 1][...].astype(F32), axis=0, keepdims=True)
        )
    rows.append(jnp.zeros((out_ref.shape[0] - pairs, out_ref.shape[1]), F32))
    out_ref[...] = jnp.concatenate(rows, axis=0).astype(BF16)


def scale_kernel(buckets, columns, own_ref, near_ref, far_ref, *refs):
    positive = (
        own_ref[...].astype(F32) + near_ref[...].astype(F32) + far_ref[0].astype(F32) + far_ref[1].astype(F32)
    )
    slope = -jax.nn.sigmoid(-positive)
    last = buckets - 1
    targets, product, riders = refs[:buckets], refs[buckets], refs[buckets + 1 : -buckets - 2]
    slope_ref, outs = refs[-buckets - 2], refs[-buckets - 1 :]
    slope_ref[...] = slope
    for bucket in range(buckets):
        outs[bucket][...] = (slope[bucket : bucket + 1] * targets[bucket][...].astype(F32)).astype(BF16)
    outs[buckets][...] = (slope[last : last + 1] * product[...].astype(F32)).astype(BF16)
    for k, out_ref in enumerate(outs[1:last] + outs[buckets:]):
        if riders:
            value = out_ref[...].astype(F32)
            rows = [value[:columns]]
            for rider in riders:
                block = rider[k].astype(F32)
                rows += [lane_row(block[k : k + 8]) for k in range(0, PACK, 8)]
            rows.append(value[columns + 2 * len(riders) :])
            out_ref[...] = jnp.concatenate(rows, axis=0).astype(BF16)


def rider_blocks(pull_ref, columns, count):
    rows = pull_ref[...].astype(F32)[columns : columns + 2 * count]
    blocks = []
    for at in range(count):
        lines_of = [
            rows[2 * at + part : 2 * at + part + 1, k * LANES : (k + 1) * LANES] for part in range(2) for k in range(8)
        ]
        blocks.append(jnp.concatenate(lines_of, axis=0).astype(BF16))
    return blocks


def source_values(total, relation_ref):
    rel = relation_ref[...].astype(F32)
    pad = rel.shape[0] // 2
    t0, t1, r0, r1 = total[:pad], total[pad:], rel[:pad], rel[pad:]
    return jnp.concatenate([t0 * r0 + t1 * r1, t1 * r0 - t0 * r1], axis=0).astype(BF16)


def write_columns(cols, rows):
    at = 0
    for row in rows:
        for k in range(0, row.shape[1], LANES):
            cols[at : at + LANES, :] = jnp.broadcast_to(row[:, k : k + LANES], (LANES, LANES)).T
            at += LANES


def scattered(values, cols, base):
    lane = lax.broadcasted_iota(I32, cols.shape, 1)
    ids = cols[...]
    hot = jnp.concatenate([(ids == lane + (base + k)).astype(BF16) for k in range(0, TILE, LANES)], axis=1)
    return jnp.dot(values[...], hot, preferred_element_type=F32)


def fill(values, cols, columns_of, rows):
    at = 0
    for value in columns_of:
        values[:, at : at + value.shape[1]] = value
        at += value.shape[1]
    write_columns(cols, rows)


def scatter_all(out_ref, values, cols, held_ref=None):
    for tile in range(out_ref.shape[1] // TILE):
        spot = slice(tile * TILE, (tile + 1) * TILE)
        total = scattered(values, cols, tile * TILE)
        out_ref[:, spot] = total if held_ref is None else total + held_ref[:, spot]


def home_kernel(ids_ref, asked_ref, slope_ref, query_ref, *refs):
    out_ref, values, cols = refs[-3:]
    buckets, edges = asked_ref.shape
    last = buckets - 1
    products, pulls, relation_rows = refs[:last], refs[last : last + 2], refs[last + 2 : last + 4]
    columns_of = [
        (slope_ref[bucket : bucket + 1] * products[bucket][...].astype(F32)).astype(BF16) for bucket in range(last)
    ]
    rows = [asked_ref[bucket : bucket + 1, :] for bucket in range(last)]
    for bucket, pull, rel in zip((0, last), pulls, relation_rows):
        query = query_ref[:, bucket * edges : (bucket + 1) * edges]
        columns_of.append(source_values(pull[...].astype(F32) + query, rel))
        rows.append(ids_ref[bucket : bucket + 1, :])
    fill(values, cols, columns_of, rows)
    scatter_all(out_ref, values, cols)


def middle_kernel(ids_ref, query_ref, *refs):
    held_ref, out_ref, values, cols = refs[-4:]
    count = (len(refs) - 4) // 2
    relation_rows, pulls = refs[:count], refs[count : 2 * count]
    edges = pulls[0].shape[1]
    columns_of, rows = [], []
    for k in range(count):
        query = query_ref[:, (k + 1) * edges : (k + 2) * edges]
        columns_of.append(source_values(pulls[k][...].astype(F32) + query, relation_rows[k]))
        rows.append(ids_ref[k + 1 : k + 2, :])
    fill(values, cols, columns_of, rows)
    scatter_all(out_ref, values, cols, held_ref)


def final_kernel(plan, origins, pos_ref, asked_ref, served_ref, push_ref, *refs):
    held_ref, out_ref, values, cols, back = refs[-5:]
    buckets, edges = asked_ref.shape
    others = refs[:-5]
    step = pl.program_id(0)
    height = push_ref.shape[0]
    pad = height // 2
    columns, lines_here, _ = out_ref.shape
    flat = out_ref.reshape(columns * lines_here, LANES)

    @pl.when(step == 0)
    def _():
        me = pos_ref[0]
        size = back.shape[0]
        if plan is not None:
            carriers, hop, left = plan
            pulls, home, direct = others[: len(carriers) - 1], others[len(carriers) - 1], others[len(carriers) :]
            back[me] = home[0]
            for carrier, ref in zip(carriers, (*pulls, push_ref)):
                for block, way in zip(rider_blocks(ref, columns, 2), (carrier, carrier + hop)):
                    back[lax.rem(me + 2 * size - way, size)] = block
            for way, ref in zip(left, direct):
                back[lax.rem(me + size - way, size)] = ref[0]
        else:
            blocks = [part[k, 0] for part in others for k in range(part.shape[0])]
            for origin, block in zip(origins, blocks):
                back[me ^ origin] = block
        returned = back[...].reshape(-1, LANES).astype(F32).T[:height].astype(BF16)
        fill(values, cols, [push_ref[...], returned], [asked_ref[buckets - 1 : buckets, :], served_ref[...]])

    tiles = lines_here * LANES // (2 * TILE)
    for tile in range(tiles):
        base = pl.multiple_of((step * tiles + tile) * TILE, TILE)
        total = scattered(values, cols, base) + held_ref[:, pl.ds(base, TILE)]
        for k in range(TILE // LANES):
            for half in range(2):
                row = 2 * (tile * (TILE // LANES) + k) + half
                flat[pl.ds(row, columns, stride=lines_here), :] = total[
                    half * pad : half * pad + columns, k * LANES : (k + 1) * LANES
                ]


def body(embeddings, relations, source_ids, relation_ids, target_ids, negative_ids, served_rows):
    halves, columns, entities = embeddings.shape
    buckets, edges = source_ids.shape
    relation_count = relations.shape[2]
    size = lax.axis_size("dom")
    height = -(-columns // 8) * 16
    pool_count = served_rows.size
    position = jnp.stack([lax.axis_index("dom"), lax.axis_index("col") & 1]).astype(I32)
    smem = pl.BlockSpec(memory_space=pltpu.SMEM)
    vmem = pl.BlockSpec(memory_space=pltpu.VMEM)
    anywhere = pl.BlockSpec(memory_space=pl.ANY)
    packet_rows = PACK + 2 * edges // LANES
    limit = VMEM_BASE + pool_count * VMEM_PER_POOL_ROW

    def local(kernel, out, *args, scratch=(), flops=0, grid=None, out_specs=None, specs=None):
        outs = out if isinstance(out, tuple) else (out,)
        chosen = [smem if a is position else vmem for a in args]
        for place, spec in (specs or {}).items():
            chosen[place] = spec
        extra = {} if grid is None else {"grid": grid}
        return pl.pallas_call(
            kernel,
            out_shape=out,
            in_specs=chosen,
            out_specs=jax.tree.map(lambda _: vmem, out) if out_specs is None else out_specs,
            scratch_shapes=list(scratch),
            compiler_params=pltpu.CompilerParams(vmem_limit_bytes=limit),
            cost_estimate=pl.CostEstimate(
                flops=int(flops),
                bytes_accessed=int(sum(a.size * a.dtype.itemsize for a in args + outs)),
                transcendentals=0,
            ),
            **extra,
        )(*args)

    edge_rows = struct(height, edges)
    gather_flops = 2 * LANES * entities * edges
    ids = jnp.concatenate(
        [source_ids, relation_ids, target_ids, jnp.pad(served_rows, ((0, 0), (0, edges - served_rows.shape[1])))],
        axis=0,
    )
    emb_lines, rel_lines = lines(embeddings), lines(relations)
    rel = local(
        relation_kernel, struct(height, relation_count), rel_lines, scratch=(pltpu.VMEM(rel_lines.shape, F32),)
    )
    emb, packet, served = local(
        functools.partial(prepare_kernel, buckets, served_rows.shape[1]),
        (struct(height, entities), struct(size, packet_rows, LANES), struct(1, pool_count, dtype=I32)),
        position, ids, emb_lines, rel,
        specs={3: anywhere},
        scratch=(
            pltpu.VMEM(emb_lines.shape, F32),
            pltpu.VMEM((buckets, packet_rows - PACK, LANES), BF16),
        ),
        flops=2 * LANES * entities * pool_count,
    )
    packet = lax.all_to_all(packet, "dom", split_axis=0, concat_axis=0, tiled=True)
    pool, asked = local(
        functools.partial(settle_kernel, 2 * buckets),
        (struct(pool_count, LANES), struct(buckets, edges, dtype=I32)),
        position, ids, packet,
    )
    made = local(product_kernel, (edge_rows,) * (2 * buckets), emb, rel, ids, flops=gather_flops * buckets)
    products, relation_rows = made[:buckets], made[buckets:]
    last = buckets - 1

    def take_targets(chosen, *after):
        return local(
            functools.partial(target_kernel, chosen), (edge_rows,) * len(chosen), emb, asked, *after,
            specs={2 + k: anywhere for k in range(len(after))},
            flops=gather_flops * len(chosen),
        )

    owned_products = [products[0]] + [rotate(products[b], "dom", -b) for b in range(1, last)]
    (last_target,) = take_targets((last,))
    last_target = rotate(last_target, "dom", last)
    width = buckets // 2 * edges
    pieces = 2
    piece = struct(pool_count, width // pieces)
    mine, *theirs = local(
        functools.partial(score_kernel, buckets),
        (struct(pool_count, width, dtype=F32),) + (piece,) * pieces,
        position, pool, *products,
        flops=2 * LANES * pool_count * edges * buckets,
    )
    pair = local(pair_kernel, (piece,) * pieces, mine, *[swap(part, "col", 1) for part in theirs])
    targets = [*take_targets(tuple(range(last))), last_target]
    after = [targets[0], *owned_products[1:], last_target]
    slopes_mine = local(
        functools.partial(slope_kernel, pieces), struct(pool_count, width),
        position, negative_ids, *pair, *[swap(part, "col", 2) for part in pair], *after,
        specs={2 + 2 * pieces + k: anywhere for k in range(len(after))},
    )
    slopes_theirs = swap(slopes_mine, "col", 1)
    pairs = [x for b in range(last) for x in (owned_products[b], targets[b])] + [products[last], last_target]
    own = local(positive_kernel, struct(PACK, edges), *pairs)
    near = swap(own, "col", 1)
    far = swap(jnp.stack([own, near]), "col", 2)
    plan = None
    groups = [list(range(size // 2)), list(range(size // 2, size))]
    if size == 2 * buckets and columns + 4 <= height // 2:
        carriers = [*range(1, last), size - last]

        def left_of(hop):
            return sorted(set(range(1, size)) - set(carriers) - {(hop + c) % size for c in carriers})

        hop = min(range(1, size), key=lambda h: len(left_of(h)))
        plan = (tuple(carriers), hop, tuple(left_of(hop)))
        groups = [[0], carriers, [hop + c for c in carriers]] + [[way] for way in left_of(hop)]
    *sent, query = local(
        functools.partial(pool_grad_kernel, buckets, groups, plan is not None),
        tuple(struct(len(group), PACK, LANES) for group in groups)
        + (struct(height, buckets * edges, dtype=F32),),
        position, slopes_mine, slopes_theirs, pool, *products,
        scratch=(pltpu.VMEM((size, PACK, LANES), BF16),),
        flops=4 * LANES * pool_count * edges * buckets,
    )
    if plan is None:
        riders, origins = (), None
        parts, origins = exchange(*sent, "dom")
    else:
        riders, origins = (sent[1], rotate(sent[2], "dom", hop)), None
        direct = [rotate(block, "dom", way) for way, block in zip(plan[2], sent[3:])]
    slope, *scaled = local(
        functools.partial(scale_kernel, buckets, columns),
        (struct(PACK, edges, dtype=F32),) + (edge_rows,) * (buckets + 1),
        own, near, far, *targets, products[last], *riders,
    )
    pulls = [rotate(scaled[b], "dom", b) for b in range(1, last)]
    push = rotate(scaled[buckets], "dom", -last)
    if plan is not None:
        parts = (*pulls, sent[0], *direct)
    count = (buckets + 1) * edges
    held = local(
        home_kernel,
        struct(height, entities, dtype=F32),
        ids, asked, slope, query, *owned_products, scaled[0], scaled[last], relation_rows[0], relation_rows[last],
        scratch=(pltpu.VMEM((height, count), BF16), pltpu.VMEM((count, LANES), I32)),
    )
    count = (last - 1) * edges
    held = local(
        middle_kernel,
        struct(height, entities, dtype=F32),
        ids, query, *relation_rows[1:last], *pulls, held,
        scratch=(pltpu.VMEM((height, count), BF16), pltpu.VMEM((count, LANES), I32)),
        flops=2 * LANES * count * entities,
    )
    steps = 4
    count = edges + pool_count
    args = [position, asked, served, push, *parts, held]
    grad = local(
        functools.partial(final_kernel, plan, origins),
        struct(columns, 2 * entities // LANES, LANES, dtype=F32),
        *args,
        grid=(steps,),
        out_specs=pl.BlockSpec((columns, 2 * entities // LANES // steps, LANES), lambda i: (0, i, 0)),
        scratch=(
            pltpu.VMEM((height, count), BF16),
            pltpu.VMEM((count, LANES), I32),
            pltpu.VMEM((size, PACK, LANES), BF16),
        ),
        flops=2 * LANES * count * entities,
    )
    return from_lines(grad, halves, columns, entities)


def solution(mesh):
    placed = (
        P(None, "col", "dom"),
        P(None, "col", None),
        P(None, "dom"),
        P(None, "dom"),
        P(None, "dom"),
        P(None, "dom", None),
        P("dom", None),
    )
    return jax.shard_map(
        body, mesh=mesh, in_specs=placed, out_specs=P(None, "col", "dom"), check_vma=False
    )
```

```python
import functools

import jax
import jax.numpy as jnp
from jax import lax
from jax.experimental import pallas as pl
from jax.experimental.pallas import tpu as pltpu
from jax.sharding import PartitionSpec as P

BF16 = jnp.bfloat16
F32 = jnp.float32
I32 = jnp.int32
LANES = 128
PACK = 16
TILE = 256
VMEM_BASE = 9 << 20
VMEM_PER_POOL_ROW = 24 << 10


def rotate(shard, axis, by):
    size = lax.axis_size(axis)
    return lax.ppermute(shard, axis, [(i, (i + by) % size) for i in range(size)])


def swap(shard, axis, bit):
    size = lax.axis_size(axis)
    return lax.ppermute(shard, axis, [(i, i ^ bit) for i in range(size)])


def exchange(first, rest, axis):
    size = 2 * first.shape[0]
    half = size // 2
    parts, origins = (first[None], swap(rest, axis, half)[None]), [0, half]
    while half > 1:
        held = jnp.concatenate(parts, axis=0)
        half //= 2
        parts = (held[:, :half], swap(held[:, half:], axis, half))
        origins = origins + [origin ^ half for origin in origins]
    return parts, tuple(origins)


def struct(*shape, dtype=BF16):
    return jax.ShapeDtypeStruct(shape, dtype)


def hot_rows(count, ids):
    return (lax.broadcasted_iota(I32, (count, ids.shape[1]), 0) == ids).astype(BF16)


def lane_row(block):
    return jnp.concatenate([block[k : k + 1, :] for k in range(block.shape[0])], axis=1)


def lines(array):
    halves, columns, count = array.shape
    cut = array.reshape(halves, columns, count // LANES, LANES)
    return cut.transpose(1, 2, 0, 3).reshape(-1, LANES)


def from_lines(array, halves, columns, count):
    cut = array.reshape(columns, count // LANES, halves, LANES)
    return cut.transpose(2, 0, 1, 3).reshape(halves, columns, count)


def unpack_lines(lines_ref, wide, out_ref):
    pad = out_ref.shape[0] // 2
    chunks = out_ref.shape[1] // LANES
    rows = lines_ref.shape[0]
    columns = rows // (2 * chunks)
    wide[:rows, :] = lines_ref[...].astype(F32)
    for k in range(chunks):
        parts = []
        for half in range(2):
            parts.append(wide[pl.ds(2 * k + half, columns, stride=2 * chunks), :])
            parts.append(jnp.zeros((pad - columns, LANES), F32))
        out_ref[:, k * LANES : (k + 1) * LANES] = jnp.concatenate(parts, axis=0).astype(BF16)


def prepare_kernel(buckets, cap, pos_ref, ids_ref, emb_ref, after_ref, embp_ref, packet_ref, row_ref, wide, coded):
    height = embp_ref.shape[0]
    me = pos_ref[0]
    edges = ids_ref.shape[1]
    for bucket in range(buckets):
        row = 2 * buckets + bucket
        block = jnp.concatenate([ids_ref[row : row + 1, k : k + LANES] for k in range(0, edges, LANES)], axis=0)
        high = lax.shift_right_logical(block, 8)
        coded[bucket] = jnp.concatenate([high, block - high * TILE], axis=0).astype(F32).astype(BF16)
    size = packet_ref.shape[0]
    row_ref[...] = jnp.concatenate(
        [ids_ref[3 * buckets + k : 3 * buckets + k + 1, :cap] for k in range(size)], axis=1
    )
    unpack_lines(emb_ref, wide, embp_ref)
    fetched = jnp.dot(embp_ref[...], hot_rows(embp_ref.shape[1], row_ref[...]), preferred_element_type=F32)
    fetched = jnp.concatenate([fetched, jnp.zeros((LANES - height, fetched.shape[1]), F32)], axis=0)
    packet_ref[:, :PACK, :] = fetched.T.astype(BF16).reshape(size, PACK, LANES)
    for to in range(size):
        bucket = jnp.minimum(lax.rem(me - to + size, size), buckets - 1)
        packet_ref[to, PACK:, :] = coded[bucket]


def relation_kernel(rel_ref, relp_ref, wide):
    unpack_lines(rel_ref, wide, relp_ref)


def take(rows_ref, ids):
    return jnp.dot(rows_ref[...], hot_rows(rows_ref.shape[1], ids), preferred_element_type=F32)


def make_product(emb_ref, rel_ref, ids_ref, buckets, bucket, product_ref, rows_ref):
    pad = emb_ref.shape[0] // 2
    source = take(emb_ref, ids_ref[bucket : bucket + 1, :])
    rel = take(rel_ref, ids_ref[buckets + bucket : buckets + bucket + 1, :])
    rows_ref[...] = rel.astype(BF16)
    s0, s1, r0, r1 = source[:pad], source[pad:], rel[:pad], rel[pad:]
    product_ref[...] = jnp.concatenate([s0 * r0 - s1 * r1, s0 * r1 + s1 * r0], axis=0).astype(BF16)


def product_kernel(emb_ref, rel_ref, ids_ref, *outs):
    buckets = len(outs) // 2
    for bucket in list(range(1, buckets)) + [0]:
        make_product(emb_ref, rel_ref, ids_ref, buckets, bucket, outs[bucket], outs[buckets + bucket])


def target_kernel(chosen, emb_ref, asked_ref, *refs):
    for bucket, out_ref in zip(chosen, refs[-len(chosen) :]):
        out_ref[...] = take(emb_ref, asked_ref[bucket : bucket + 1, :]).astype(BF16)


def pair_kernel(mine_ref, *refs):
    count = len(refs) // 2
    width = refs[0].shape[1]
    for k in range(count):
        spot = slice(k * width, (k + 1) * width)
        refs[count + k][...] = (mine_ref[:, spot] + refs[k][...].astype(F32)).astype(BF16)


def score_kernel(buckets, pos_ref, packet_ref, ids_ref, *refs):
    products, (pool_ref, asked_ref, mine_ref), pieces = refs[:buckets], refs[buckets : buckets + 3], refs[buckets + 3 :]
    me, core = pos_ref[0], pos_ref[1]
    size = packet_ref.shape[0]
    height, edges = products[0].shape
    per = len(pieces) // (buckets // 2)
    cut = edges // per
    packets = packet_ref[:, :PACK, :].reshape(pool_ref.shape)
    pool_ref[...] = packets
    pool = packets[:, :height]
    for bucket in range(buckets):
        half, place = divmod(bucket, buckets // 2)
        scores = jnp.dot(pool, products[bucket][...], preferred_element_type=F32)

        @pl.when(core == half)
        def _():
            mine_ref[:, place * edges : (place + 1) * edges] = scores

        @pl.when(core != half)
        def _():
            for k in range(per):
                pieces[place * per + k][...] = scores[:, k * cut : (k + 1) * cut].astype(BF16)

    asked_ref[0:1, :] = ids_ref[2 * buckets : 2 * buckets + 1, :]
    for bucket in range(1, buckets):
        coded = packet_ref[lax.rem(me + bucket, size), PACK:, :].astype(F32)
        half = coded.shape[0] // 2
        asked_ref[bucket : bucket + 1, :] = lane_row((coded[:half] * float(TILE) + coded[half:]).astype(I32))


def join_kernel(own_ref, near_ref, after_ref, out_ref):
    out_ref[0] = own_ref[...]
    out_ref[1] = near_ref[...]


def slope_kernel(pieces, pos_ref, negatives_ref, *refs):
    out_ref = refs[-1]
    core = pos_ref[1]
    count, width = refs[0].shape
    buckets, spans, negs = negatives_ref.shape
    span_len = width * pieces // (buckets // 2 * spans)
    for place in range(buckets // 2):
        for span in range(spans):
            drawn = negatives_ref[core * (buckets // 2) + place, span : span + 1, :]
            times = jnp.sum(
                (lax.broadcasted_iota(I32, (count, negs), 0) == drawn).astype(F32), axis=1, keepdims=True
            )
            start = (place * spans + span) * span_len
            piece, offset = divmod(start, width)
            spot = slice(offset, offset + span_len)
            scores = refs[piece][:, spot].astype(F32) + refs[pieces + piece][:, spot].astype(F32)
            out_ref[:, start : start + span_len] = (times * jax.nn.sigmoid(scores)).astype(BF16)


def bucket_slopes(core, mine_ref, theirs_ref, bucket, buckets, edges):
    half, place = divmod(bucket, buckets // 2)
    spot = slice(place * edges, (place + 1) * edges)
    return jnp.where(core == half, mine_ref[:, spot], theirs_ref[:, spot])


def pool_grad_kernel(buckets, groups, ring, pos_ref, mine_ref, theirs_ref, pool_ref, *refs):
    held, query_ref = refs[-1], refs[-2]
    outs = refs[-2 - len(groups) : -2]
    core = pos_ref[1]
    height, edges = refs[0].shape
    pool = pool_ref[...].astype(F32).T[:height].astype(BF16)
    total = None
    for bucket in range(buckets):
        slopes = bucket_slopes(core, mine_ref, theirs_ref, bucket, buckets, edges)
        query_ref[:, bucket * edges : (bucket + 1) * edges] = jnp.dot(pool, slopes, preferred_element_type=F32)
        part = lax.dot_general(
            slopes, refs[bucket][...], (((1,), (1,)), ((), ())), preferred_element_type=F32
        )
        total = part if total is None else total + part
    total = jnp.concatenate([total, jnp.zeros((total.shape[0], LANES - height), F32)], axis=1)
    held[...] = total.astype(BF16).reshape(held.shape)
    me = pos_ref[0]
    size = held.shape[0]
    for group, out_ref in zip(groups, outs):
        for k, offset in enumerate(group):
            out_ref[k] = held[lax.rem(me + offset, size) if ring else me ^ offset]


def positive_kernel(*refs):
    out_ref = refs[-1]
    pairs = len(refs) // 2
    rows = []
    for k in range(pairs):
        rows.append(
            jnp.sum(refs[2 * k][...].astype(F32) * refs[2 * k + 1][...].astype(F32), axis=0, keepdims=True)
        )
    rows.append(jnp.zeros((out_ref.shape[0] - pairs, out_ref.shape[1]), F32))
    out_ref[...] = jnp.concatenate(rows, axis=0).astype(BF16)


def scale_kernel(buckets, columns, count, own_ref, near_ref, far_ref, *refs):
    positive = (
        own_ref[...].astype(F32) + near_ref[...].astype(F32) + far_ref[0].astype(F32) + far_ref[1].astype(F32)
    )
    slope = -jax.nn.sigmoid(-positive)
    last = buckets - 1
    targets, product, riders = refs[:buckets], refs[buckets], refs[buckets + 1 : buckets + 1 + count]
    slope_ref, outs = refs[-buckets - 2], refs[-buckets - 1 :]
    slope_ref[...] = slope
    for bucket in range(buckets):
        outs[bucket][...] = (slope[bucket : bucket + 1] * targets[bucket][...].astype(F32)).astype(BF16)
    outs[buckets][...] = (slope[last : last + 1] * product[...].astype(F32)).astype(BF16)
    for k, out_ref in enumerate(outs[1:last] + outs[buckets:]):
        if riders:
            value = out_ref[...].astype(F32)
            rows = [value[:columns]]
            for rider in riders:
                block = rider[k].astype(F32)
                rows += [lane_row(block[k : k + 8]) for k in range(0, PACK, 8)]
            rows.append(value[columns + 2 * len(riders) :])
            out_ref[...] = jnp.concatenate(rows, axis=0).astype(BF16)


def rider_blocks(pull_ref, columns, count):
    rows = pull_ref[...].astype(F32)[columns : columns + 2 * count]
    blocks = []
    for at in range(count):
        lines_of = [
            rows[2 * at + part : 2 * at + part + 1, k * LANES : (k + 1) * LANES] for part in range(2) for k in range(8)
        ]
        blocks.append(jnp.concatenate(lines_of, axis=0).astype(BF16))
    return blocks


def source_values(total, relation_ref):
    rel = relation_ref[...].astype(F32)
    pad = rel.shape[0] // 2
    t0, t1, r0, r1 = total[:pad], total[pad:], rel[:pad], rel[pad:]
    return jnp.concatenate([t0 * r0 + t1 * r1, t1 * r0 - t0 * r1], axis=0).astype(BF16)


def write_columns(cols, rows):
    at = 0
    for row in rows:
        for k in range(0, row.shape[1], LANES):
            cols[at : at + LANES, :] = jnp.broadcast_to(row[:, k : k + LANES], (LANES, LANES)).T
            at += LANES


def scattered(values, cols, base):
    lane = lax.broadcasted_iota(I32, cols.shape, 1)
    ids = cols[...]
    hot = jnp.concatenate([(ids == lane + (base + k)).astype(BF16) for k in range(0, TILE, LANES)], axis=1)
    return jnp.dot(values[...], hot, preferred_element_type=F32)


def fill(values, cols, columns_of, rows):
    at = 0
    for value in columns_of:
        values[:, at : at + value.shape[1]] = value
        at += value.shape[1]
    write_columns(cols, rows)


def scatter_all(out_ref, values, cols, held_ref=None):
    for tile in range(out_ref.shape[1] // TILE):
        spot = slice(tile * TILE, (tile + 1) * TILE)
        total = scattered(values, cols, tile * TILE)
        out_ref[:, spot] = total if held_ref is None else total + held_ref[:, spot]


def home_kernel(ids_ref, asked_ref, slope_ref, query_ref, *refs):
    out_ref, values, cols = refs[-3:]
    buckets, edges = asked_ref.shape
    last = buckets - 1
    products, pulls, relation_rows = refs[:last], refs[last : last + 2], refs[last + 2 : last + 4]
    columns_of = [
        (slope_ref[bucket : bucket + 1] * products[bucket][...].astype(F32)).astype(BF16) for bucket in range(last)
    ]
    rows = [asked_ref[bucket : bucket + 1, :] for bucket in range(last)]
    for bucket, pull, rel in zip((0, last), pulls, relation_rows):
        query = query_ref[:, bucket * edges : (bucket + 1) * edges]
        columns_of.append(source_values(pull[...].astype(F32) + query, rel))
        rows.append(ids_ref[bucket : bucket + 1, :])
    fill(values, cols, columns_of, rows)
    scatter_all(out_ref, values, cols)


def middle_kernel(ids_ref, query_ref, *refs):
    held_ref, out_ref, values, cols = refs[-4:]
    count = (len(refs) - 4) // 2
    relation_rows, pulls = refs[:count], refs[count : 2 * count]
    edges = pulls[0].shape[1]
    columns_of, rows = [], []
    for k in range(count):
        query = query_ref[:, (k + 1) * edges : (k + 2) * edges]
        columns_of.append(source_values(pulls[k][...].astype(F32) + query, relation_rows[k]))
        rows.append(ids_ref[k + 1 : k + 2, :])
    fill(values, cols, columns_of, rows)
    scatter_all(out_ref, values, cols, held_ref)


def final_kernel(plan, origins, pos_ref, asked_ref, served_ref, push_ref, *refs):
    held_ref, out_hbm, values, cols, back, out_ref, sems = refs[-7:]
    buckets, edges = asked_ref.shape
    others = refs[:-7]
    height = push_ref.shape[0]
    pad = height // 2
    steps, columns, lines_here, _ = out_ref.shape
    me = pos_ref[0]
    size = back.shape[0]
    if plan is not None:
        carriers, hop, left = plan
        pulls, home, direct = others[: len(carriers) - 1], others[len(carriers) - 1], others[len(carriers) :]
        back[me] = home[0]
        for carrier, ref in zip(carriers, (*pulls, push_ref)):
            for block, way in zip(rider_blocks(ref, columns, 2), (carrier, carrier + hop)):
                back[lax.rem(me + 2 * size - way, size)] = block
        for way, ref in zip(left, direct):
            back[lax.rem(me + size - way, size)] = ref[0]
    else:
        blocks = [part[k, 0] for part in others for k in range(part.shape[0])]
        for origin, block in zip(origins, blocks):
            back[me ^ origin] = block
    returned = back[...].reshape(-1, LANES).astype(F32).T[:height].astype(BF16)
    fill(values, cols, [push_ref[...], returned], [asked_ref[buckets - 1 : buckets, :], served_ref[...]])

    tiles = lines_here * LANES // (2 * TILE)
    copies = []
    for step in range(steps):
        flat = out_ref.at[step].reshape(columns * lines_here, LANES)
        for tile in range(tiles):
            base = (step * tiles + tile) * TILE
            total = scattered(values, cols, base) + held_ref[:, base : base + TILE]
            for k in range(TILE // LANES):
                for half in range(2):
                    row = 2 * (tile * (TILE // LANES) + k) + half
                    flat[pl.ds(row, columns, stride=lines_here), :] = total[
                        half * pad : half * pad + columns, k * LANES : (k + 1) * LANES
                    ]
        there = out_hbm.at[:, step * lines_here : (step + 1) * lines_here, :]
        copies.append(pltpu.make_async_copy(out_ref.at[step], there, sems.at[step]))
        copies[-1].start()
    for copy in copies:
        copy.wait()


def body(embeddings, relations, source_ids, relation_ids, target_ids, negative_ids, served_rows):
    halves, columns, entities = embeddings.shape
    buckets, edges = source_ids.shape
    relation_count = relations.shape[2]
    size = lax.axis_size("dom")
    height = -(-columns // 8) * 16
    pool_count = served_rows.size
    position = jnp.stack([lax.axis_index("dom"), lax.axis_index("col") & 1]).astype(I32)
    smem = pl.BlockSpec(memory_space=pltpu.SMEM)
    vmem = pl.BlockSpec(memory_space=pltpu.VMEM)
    anywhere = pl.BlockSpec(memory_space=pl.ANY)
    packet_rows = PACK + 2 * edges // LANES
    limit = VMEM_BASE + pool_count * VMEM_PER_POOL_ROW

    def local(kernel, out, *args, scratch=(), flops=0, grid=None, out_specs=None, specs=None):
        outs = out if isinstance(out, tuple) else (out,)
        chosen = [smem if a is position else vmem for a in args]
        for place, spec in (specs or {}).items():
            chosen[place] = spec
        extra = {} if grid is None else {"grid": grid}
        return pl.pallas_call(
            kernel,
            out_shape=out,
            in_specs=chosen,
            out_specs=jax.tree.map(lambda _: vmem, out) if out_specs is None else out_specs,
            scratch_shapes=list(scratch),
            compiler_params=pltpu.CompilerParams(vmem_limit_bytes=limit),
            cost_estimate=pl.CostEstimate(
                flops=int(flops),
                bytes_accessed=int(sum(a.size * a.dtype.itemsize for a in args + outs)),
                transcendentals=0,
            ),
            **extra,
        )(*args)

    edge_rows = struct(height, edges)
    gather_flops = 2 * LANES * entities * edges
    ids = jnp.concatenate(
        [source_ids, relation_ids, target_ids, jnp.pad(served_rows, ((0, 0), (0, edges - served_rows.shape[1])))],
        axis=0,
    )
    emb_lines, rel_lines = lines(embeddings), lines(relations)
    rel = local(
        relation_kernel, struct(height, relation_count), rel_lines, scratch=(pltpu.VMEM(rel_lines.shape, F32),)
    )
    emb, packet, served = local(
        functools.partial(prepare_kernel, buckets, served_rows.shape[1]),
        (struct(height, entities), struct(size, packet_rows, LANES), struct(1, pool_count, dtype=I32)),
        position, ids, emb_lines, rel,
        specs={3: anywhere},
        scratch=(
            pltpu.VMEM(emb_lines.shape, F32),
            pltpu.VMEM((buckets, packet_rows - PACK, LANES), BF16),
        ),
        flops=2 * LANES * entities * pool_count,
    )
    packet = lax.all_to_all(packet, "dom", split_axis=0, concat_axis=0, tiled=True)
    made = local(product_kernel, (edge_rows,) * (2 * buckets), emb, rel, ids, flops=gather_flops * buckets)
    products, relation_rows = made[:buckets], made[buckets:]
    last = buckets - 1

    def take_targets(chosen, *after):
        return local(
            functools.partial(target_kernel, chosen), (edge_rows,) * len(chosen), emb, asked, *after,
            specs={2 + k: anywhere for k in range(len(after))},
            flops=gather_flops * len(chosen),
        )

    owned_products = [products[0]] + [rotate(products[b], "dom", -b) for b in range(1, last)]
    width = buckets // 2 * edges
    pieces = 2
    piece = struct(pool_count, width // pieces)
    pool, asked, mine, *theirs = local(
        functools.partial(score_kernel, buckets),
        (
            struct(pool_count, LANES),
            struct(buckets, edges, dtype=I32),
            struct(pool_count, width, dtype=F32),
            *(piece,) * pieces,
        ),
        position, packet, ids, *products,
        flops=2 * LANES * pool_count * edges * buckets,
    )
    (last_target,) = take_targets((last,))
    last_target = rotate(last_target, "dom", last)
    pair = local(pair_kernel, (piece,) * pieces, mine, *[swap(part, "col", 1) for part in theirs])
    targets = [*take_targets(tuple(range(last))), last_target]
    after = [targets[0], *owned_products[1:], last_target]
    slopes_mine = local(
        functools.partial(slope_kernel, pieces), struct(pool_count, width),
        position, negative_ids, *pair, *[swap(part, "col", 2) for part in pair], *after,
        specs={2 + 2 * pieces + k: anywhere for k in range(len(after))},
    )
    slopes_theirs = swap(slopes_mine, "col", 1)
    pairs = [x for b in range(last) for x in (owned_products[b], targets[b])] + [products[last], last_target]
    own = local(positive_kernel, struct(PACK, edges), *pairs)
    near = swap(own, "col", 1)
    plan = None
    groups = [list(range(size // 2)), list(range(size // 2, size))]
    if size == 2 * buckets and columns + 4 <= height // 2:
        carriers = [*range(1, last), size - last]

        def left_of(hop):
            return sorted(set(range(1, size)) - set(carriers) - {(hop + c) % size for c in carriers})

        hop = min(range(1, size), key=lambda h: len(left_of(h)))
        plan = (tuple(carriers), hop, tuple(left_of(hop)))
        groups = [[0], carriers, [hop + c for c in carriers]] + [[way] for way in left_of(hop)]
    *sent, query = local(
        functools.partial(pool_grad_kernel, buckets, groups, plan is not None),
        tuple(struct(len(group), PACK, LANES) for group in groups)
        + (struct(height, buckets * edges, dtype=F32),),
        position, slopes_mine, slopes_theirs, pool, *products,
        scratch=(pltpu.VMEM((size, PACK, LANES), BF16),),
        flops=4 * LANES * pool_count * edges * buckets,
    )
    joined = local(
        join_kernel, struct(2, PACK, edges), own, near, query, specs={2: anywhere}
    )
    far = swap(joined, "col", 2)
    if plan is None:
        riders, direct = (), ()
        parts, origins = exchange(*sent, "dom")
    else:
        riders, origins = (sent[1], rotate(sent[2], "dom", hop)), None
        direct = [rotate(block, "dom", way) for way, block in zip(plan[2], sent[3:])]
    slope, *scaled = local(
        functools.partial(scale_kernel, buckets, columns, len(riders)),
        (struct(PACK, edges, dtype=F32),) + (edge_rows,) * (buckets + 1),
        own, near, far, *targets, products[last], *riders,
    )
    pulls = [rotate(scaled[b], "dom", b) for b in range(1, last)]
    push = rotate(scaled[buckets], "dom", -last)
    if plan is not None:
        parts = (*pulls, sent[0], *direct)
    count = (buckets + 1) * edges
    held = local(
        home_kernel,
        struct(height, entities, dtype=F32),
        ids, asked, slope, query, *owned_products, scaled[0], scaled[last], relation_rows[0], relation_rows[last],
        scratch=(pltpu.VMEM((height, count), BF16), pltpu.VMEM((count, LANES), I32)),
    )
    count = (last - 1) * edges
    held = local(
        middle_kernel,
        struct(height, entities, dtype=F32),
        ids, query, *relation_rows[1:last], *pulls, held,
        scratch=(pltpu.VMEM((height, count), BF16), pltpu.VMEM((count, LANES), I32)),
        flops=2 * LANES * count * entities,
    )
    steps = 8
    count = edges + pool_count
    args = [position, asked, served, push, *parts, held]
    grad = local(
        functools.partial(final_kernel, plan, origins),
        struct(columns, 2 * entities // LANES, LANES, dtype=F32),
        *args,
        out_specs=anywhere,
        scratch=(
            pltpu.VMEM((height, count), BF16),
            pltpu.VMEM((count, LANES), I32),
            pltpu.VMEM((size, PACK, LANES), BF16),
            pltpu.VMEM((steps, columns, 2 * entities // LANES // steps, LANES), F32),
            pltpu.SemaphoreType.DMA((steps,)),
        ),
        flops=2 * LANES * count * entities,
    )
    return from_lines(grad, halves, columns, entities)


def solution(mesh):
    placed = (
        P(None, "col", "dom"),
        P(None, "col", None),
        P(None, "dom"),
        P(None, "dom"),
        P(None, "dom"),
        P(None, "dom", None),
        P("dom", None),
    )
    return jax.shard_map(
        body, mesh=mesh, in_specs=placed, out_specs=P(None, "col", "dom"), check_vma=False
    )
```

```python
import functools

import jax
import jax.numpy as jnp
from jax import lax
from jax.experimental import pallas as pl
from jax.experimental.pallas import tpu as pltpu
from jax.sharding import PartitionSpec as P

BF16 = jnp.bfloat16
F32 = jnp.float32
I32 = jnp.int32
LANES = 128
PACK = 16
TILE = 256
VMEM_BASE = 9 << 20
VMEM_PER_POOL_ROW = 24 << 10


def rotate(shard, axis, by):
    size = lax.axis_size(axis)
    return lax.ppermute(shard, axis, [(i, (i + by) % size) for i in range(size)])


def swap(shard, axis, bit):
    size = lax.axis_size(axis)
    return lax.ppermute(shard, axis, [(i, i ^ bit) for i in range(size)])


def exchange(first, rest, axis):
    size = 2 * first.shape[0]
    half = size // 2
    parts, origins = (first[None], swap(rest, axis, half)[None]), [0, half]
    while half > 1:
        held = jnp.concatenate(parts, axis=0)
        half //= 2
        parts = (held[:, :half], swap(held[:, half:], axis, half))
        origins = origins + [origin ^ half for origin in origins]
    return parts, tuple(origins)


def struct(*shape, dtype=BF16):
    return jax.ShapeDtypeStruct(shape, dtype)


def hot_rows(count, ids):
    return (lax.broadcasted_iota(I32, (count, ids.shape[1]), 0) == ids).astype(BF16)


def lane_row(block):
    return jnp.concatenate([block[k : k + 1, :] for k in range(block.shape[0])], axis=1)


def lines(array):
    halves, columns, count = array.shape
    cut = array.reshape(halves, columns, count // LANES, LANES)
    return cut.transpose(1, 2, 0, 3).reshape(-1, LANES)


def from_lines(array, halves, columns, count):
    cut = array.reshape(columns, count // LANES, halves, LANES)
    return cut.transpose(2, 0, 1, 3).reshape(halves, columns, count)


def unpack_lines(lines_ref, wide, out_ref):
    pad = out_ref.shape[0] // 2
    chunks = out_ref.shape[1] // LANES
    rows = lines_ref.shape[0]
    columns = rows // (2 * chunks)
    wide[:rows, :] = lines_ref[...].astype(F32)
    for k in range(chunks):
        parts = []
        for half in range(2):
            parts.append(wide[pl.ds(2 * k + half, columns, stride=2 * chunks), :])
            parts.append(jnp.zeros((pad - columns, LANES), F32))
        out_ref[:, k * LANES : (k + 1) * LANES] = jnp.concatenate(parts, axis=0).astype(BF16)


def prepare_kernel(buckets, cap, pos_ref, ids_ref, emb_ref, after_ref, embp_ref, packet_ref, row_ref, wide, coded):
    height = embp_ref.shape[0]
    me = pos_ref[0]
    edges = ids_ref.shape[1]
    for bucket in range(buckets):
        row = 2 * buckets + bucket
        block = jnp.concatenate([ids_ref[row : row + 1, k : k + LANES] for k in range(0, edges, LANES)], axis=0)
        high = lax.shift_right_logical(block, 8)
        coded[bucket] = jnp.concatenate([high, block - high * TILE], axis=0).astype(F32).astype(BF16)
    size = packet_ref.shape[0]
    row_ref[...] = jnp.concatenate(
        [ids_ref[3 * buckets + k : 3 * buckets + k + 1, :cap] for k in range(size)], axis=1
    )
    unpack_lines(emb_ref, wide, embp_ref)
    fetched = jnp.dot(embp_ref[...], hot_rows(embp_ref.shape[1], row_ref[...]), preferred_element_type=F32)
    fetched = jnp.concatenate([fetched, jnp.zeros((LANES - height, fetched.shape[1]), F32)], axis=0)
    packet_ref[:, :PACK, :] = fetched.T.astype(BF16).reshape(size, PACK, LANES)
    for to in range(size):
        bucket = jnp.minimum(lax.rem(me - to + size, size), buckets - 1)
        packet_ref[to, PACK:, :] = coded[bucket]


def relation_kernel(rel_ref, relp_ref, wide):
    unpack_lines(rel_ref, wide, relp_ref)


def take(rows_ref, ids):
    return jnp.dot(rows_ref[...], hot_rows(rows_ref.shape[1], ids), preferred_element_type=F32)


def make_product(emb_ref, rel_ref, ids_ref, buckets, bucket, product_ref, rows_ref):
    pad = emb_ref.shape[0] // 2
    source = take(emb_ref, ids_ref[bucket : bucket + 1, :])
    rel = take(rel_ref, ids_ref[buckets + bucket : buckets + bucket + 1, :])
    rows_ref[...] = rel.astype(BF16)
    s0, s1, r0, r1 = source[:pad], source[pad:], rel[:pad], rel[pad:]
    product_ref[...] = jnp.concatenate([s0 * r0 - s1 * r1, s0 * r1 + s1 * r0], axis=0).astype(BF16)


def product_kernel(emb_ref, rel_ref, ids_ref, *outs):
    buckets = len(outs) // 2
    for bucket in list(range(1, buckets)) + [0]:
        make_product(emb_ref, rel_ref, ids_ref, buckets, bucket, outs[bucket], outs[buckets + bucket])


def target_kernel(chosen, emb_ref, asked_ref, *refs):
    for bucket, out_ref in zip(chosen, refs[-len(chosen) :]):
        out_ref[...] = take(emb_ref, asked_ref[bucket : bucket + 1, :]).astype(BF16)


def pair_kernel(mine_ref, *refs):
    count = len(refs) // 2
    width = refs[0].shape[1]
    for k in range(count):
        spot = slice(k * width, (k + 1) * width)
        refs[count + k][...] = (mine_ref[:, spot] + refs[k][...].astype(F32)).astype(BF16)


def score_kernel(buckets, pos_ref, packet_ref, ids_ref, *refs):
    products, (pool_ref, asked_ref, mine_ref), pieces = refs[:buckets], refs[buckets : buckets + 3], refs[buckets + 3 :]
    me, core = pos_ref[0], pos_ref[1]
    size = packet_ref.shape[0]
    height, edges = products[0].shape
    per = len(pieces) // (buckets // 2)
    cut = edges // per
    packets = packet_ref[:, :PACK, :].reshape(pool_ref.shape)
    pool_ref[...] = packets
    pool = packets[:, :height]
    for bucket in range(buckets):
        half, place = divmod(bucket, buckets // 2)
        scores = jnp.dot(pool, products[bucket][...], preferred_element_type=F32)

        @pl.when(core == half)
        def _():
            mine_ref[:, place * edges : (place + 1) * edges] = scores

        @pl.when(core != half)
        def _():
            for k in range(per):
                pieces[place * per + k][...] = scores[:, k * cut : (k + 1) * cut].astype(BF16)

    asked_ref[0:1, :] = ids_ref[2 * buckets : 2 * buckets + 1, :]
    for bucket in range(1, buckets):
        coded = packet_ref[lax.rem(me + bucket, size), PACK:, :].astype(F32)
        half = coded.shape[0] // 2
        asked_ref[bucket : bucket + 1, :] = lane_row((coded[:half] * float(TILE) + coded[half:]).astype(I32))


def join_kernel(own_ref, near_ref, after_ref, out_ref):
    out_ref[0] = own_ref[...]
    out_ref[1] = near_ref[...]


def slope_kernel(pieces, pos_ref, negatives_ref, *refs):
    out_ref = refs[-1]
    core = pos_ref[1]
    count, width = refs[0].shape
    buckets, spans, negs = negatives_ref.shape
    span_len = width * pieces // (buckets // 2 * spans)
    for place in range(buckets // 2):
        for span in range(spans):
            drawn = negatives_ref[core * (buckets // 2) + place, span : span + 1, :]
            times = jnp.sum(
                (lax.broadcasted_iota(I32, (count, negs), 0) == drawn).astype(F32), axis=1, keepdims=True
            )
            start = (place * spans + span) * span_len
            piece, offset = divmod(start, width)
            spot = slice(offset, offset + span_len)
            scores = refs[piece][:, spot].astype(F32) + refs[pieces + piece][:, spot].astype(F32)
            out_ref[:, start : start + span_len] = (times * jax.nn.sigmoid(scores)).astype(BF16)


def bucket_slopes(core, mine_ref, theirs_ref, bucket, buckets, edges):
    half, place = divmod(bucket, buckets // 2)
    spot = slice(place * edges, (place + 1) * edges)
    return jnp.where(core == half, mine_ref[:, spot], theirs_ref[:, spot])


def pool_grad_kernel(buckets, groups, ring, pos_ref, mine_ref, theirs_ref, pool_ref, *refs):
    held, query_ref = refs[-1], refs[-2]
    outs = refs[-2 - len(groups) : -2]
    core = pos_ref[1]
    height, edges = refs[0].shape
    pool = pool_ref[...].astype(F32).T[:height].astype(BF16)
    total = None
    for bucket in range(buckets):
        slopes = bucket_slopes(core, mine_ref, theirs_ref, bucket, buckets, edges)
        query_ref[:, bucket * edges : (bucket + 1) * edges] = jnp.dot(pool, slopes, preferred_element_type=F32)
        part = lax.dot_general(
            slopes, refs[bucket][...], (((1,), (1,)), ((), ())), preferred_element_type=F32
        )
        total = part if total is None else total + part
    total = jnp.concatenate([total, jnp.zeros((total.shape[0], LANES - height), F32)], axis=1)
    held[...] = total.astype(BF16).reshape(held.shape)
    me = pos_ref[0]
    size = held.shape[0]
    for group, out_ref in zip(groups, outs):
        for k, offset in enumerate(group):
            out_ref[k] = held[lax.rem(me + offset, size) if ring else me ^ offset]


def positive_kernel(*refs):
    out_ref = refs[-1]
    pairs = len(refs) // 2
    rows = []
    for k in range(pairs):
        rows.append(
            jnp.sum(refs[2 * k][...].astype(F32) * refs[2 * k + 1][...].astype(F32), axis=0, keepdims=True)
        )
    rows.append(jnp.zeros((out_ref.shape[0] - pairs, out_ref.shape[1]), F32))
    out_ref[...] = jnp.concatenate(rows, axis=0).astype(BF16)


def scale_kernel(buckets, columns, count, own_ref, near_ref, far_ref, *refs):
    positive = (
        own_ref[...].astype(F32) + near_ref[...].astype(F32) + far_ref[0].astype(F32) + far_ref[1].astype(F32)
    )
    slope = -jax.nn.sigmoid(-positive)
    last = buckets - 1
    targets, product, riders = refs[:buckets], refs[buckets], refs[buckets + 1 : buckets + 1 + count]
    slope_ref, outs = refs[-buckets - 2], refs[-buckets - 1 :]
    slope_ref[...] = slope
    for bucket in range(buckets):
        outs[bucket][...] = (slope[bucket : bucket + 1] * targets[bucket][...].astype(F32)).astype(BF16)
    outs[buckets][...] = (slope[last : last + 1] * product[...].astype(F32)).astype(BF16)
    for k, out_ref in enumerate(outs[1:last] + outs[buckets:]):
        if riders:
            value = out_ref[...].astype(F32)
            rows = [value[:columns]]
            for rider in riders:
                block = rider[k].astype(F32)
                rows += [lane_row(block[k : k + 8]) for k in range(0, PACK, 8)]
            rows.append(value[columns + 2 * len(riders) :])
            out_ref[...] = jnp.concatenate(rows, axis=0).astype(BF16)


def rider_blocks(pull_ref, columns, count):
    rows = pull_ref[...].astype(F32)[columns : columns + 2 * count]
    blocks = []
    for at in range(count):
        lines_of = [
            rows[2 * at + part : 2 * at + part + 1, k * LANES : (k + 1) * LANES] for part in range(2) for k in range(8)
        ]
        blocks.append(jnp.concatenate(lines_of, axis=0).astype(BF16))
    return blocks


def source_values(total, relation_ref):
    rel = relation_ref[...].astype(F32)
    pad = rel.shape[0] // 2
    t0, t1, r0, r1 = total[:pad], total[pad:], rel[:pad], rel[pad:]
    return jnp.concatenate([t0 * r0 + t1 * r1, t1 * r0 - t0 * r1], axis=0).astype(BF16)


def write_columns(cols, rows):
    at = 0
    for row in rows:
        for k in range(0, row.shape[1], LANES):
            cols[at : at + LANES, :] = jnp.broadcast_to(row[:, k : k + LANES], (LANES, LANES)).T
            at += LANES


def scattered(values, cols, base):
    lane = lax.broadcasted_iota(I32, cols.shape, 1)
    ids = cols[...]
    hot = jnp.concatenate([(ids == lane + (base + k)).astype(BF16) for k in range(0, TILE, LANES)], axis=1)
    return jnp.dot(values[...], hot, preferred_element_type=F32)


def fill(values, columns_of):
    at = 0
    for value in columns_of:
        values[:, at : at + value.shape[1]] = value
        at += value.shape[1]


def columns_kernel(ids_ref, asked_ref, served_ref, after_ref, home_ref, middle_ref, final_ref):
    buckets = asked_ref.shape[0]
    last = buckets - 1
    asked = [asked_ref[bucket : bucket + 1, :] for bucket in range(buckets)]
    sources = [ids_ref[bucket : bucket + 1, :] for bucket in range(buckets)]
    write_columns(home_ref, [*asked[:last], sources[0], sources[last]])
    write_columns(middle_ref, sources[1:last])
    write_columns(final_ref, [asked[last], served_ref[...]])


def scatter_all(out_ref, values, cols, held_ref=None):
    for tile in range(out_ref.shape[1] // TILE):
        spot = slice(tile * TILE, (tile + 1) * TILE)
        total = scattered(values, cols, tile * TILE)
        out_ref[:, spot] = total if held_ref is None else total + held_ref[:, spot]


def home_kernel(ids_ref, asked_ref, slope_ref, query_ref, *refs):
    cols, out_ref, values = refs[-3:]
    buckets, edges = asked_ref.shape
    last = buckets - 1
    products, pulls, relation_rows = refs[:last], refs[last : last + 2], refs[last + 2 : last + 4]
    columns_of = [
        (slope_ref[bucket : bucket + 1] * products[bucket][...].astype(F32)).astype(BF16) for bucket in range(last)
    ]
    for bucket, pull, rel in zip((0, last), pulls, relation_rows):
        query = query_ref[:, bucket * edges : (bucket + 1) * edges]
        columns_of.append(source_values(pull[...].astype(F32) + query, rel))
    fill(values, columns_of)
    scatter_all(out_ref, values, cols)


def middle_kernel(ids_ref, query_ref, *refs):
    held_ref, cols, out_ref, values = refs[-4:]
    count = (len(refs) - 4) // 2
    relation_rows, pulls = refs[:count], refs[count : 2 * count]
    edges = pulls[0].shape[1]
    columns_of = []
    for k in range(count):
        query = query_ref[:, (k + 1) * edges : (k + 2) * edges]
        columns_of.append(source_values(pulls[k][...].astype(F32) + query, relation_rows[k]))
    fill(values, columns_of)
    scatter_all(out_ref, values, cols, held_ref)


def final_kernel(plan, origins, pos_ref, asked_ref, served_ref, push_ref, *refs):
    held_ref, cols, out_hbm, values, back, out_ref, sems = refs[-7:]
    buckets, edges = asked_ref.shape
    others = refs[:-7]
    height = push_ref.shape[0]
    pad = height // 2
    steps, columns, lines_here, _ = out_ref.shape
    me = pos_ref[0]
    size = back.shape[0]
    if plan is not None:
        carriers, hop, left = plan
        pulls, home, direct = others[: len(carriers) - 1], others[len(carriers) - 1], others[len(carriers) :]
        back[me] = home[0]
        for carrier, ref in zip(carriers, (*pulls, push_ref)):
            for block, way in zip(rider_blocks(ref, columns, 2), (carrier, carrier + hop)):
                back[lax.rem(me + 2 * size - way, size)] = block
        for way, ref in zip(left, direct):
            back[lax.rem(me + size - way, size)] = ref[0]
    else:
        blocks = [part[k, 0] for part in others for k in range(part.shape[0])]
        for origin, block in zip(origins, blocks):
            back[me ^ origin] = block
    returned = back[...].reshape(-1, LANES).astype(F32).T[:height].astype(BF16)
    fill(values, [push_ref[...], returned])

    tiles = lines_here * LANES // (2 * TILE)
    copies = []
    for step in range(steps):
        flat = out_ref.at[step].reshape(columns * lines_here, LANES)
        for tile in range(tiles):
            base = (step * tiles + tile) * TILE
            total = scattered(values, cols, base) + held_ref[:, base : base + TILE]
            for k in range(TILE // LANES):
                for half in range(2):
                    row = 2 * (tile * (TILE // LANES) + k) + half
                    flat[pl.ds(row, columns, stride=lines_here), :] = total[
                        half * pad : half * pad + columns, k * LANES : (k + 1) * LANES
                    ]
        there = out_hbm.at[:, step * lines_here : (step + 1) * lines_here, :]
        copies.append(pltpu.make_async_copy(out_ref.at[step], there, sems.at[step]))
        copies[-1].start()
    for copy in copies:
        copy.wait()


def body(embeddings, relations, source_ids, relation_ids, target_ids, negative_ids, served_rows):
    halves, columns, entities = embeddings.shape
    buckets, edges = source_ids.shape
    relation_count = relations.shape[2]
    size = lax.axis_size("dom")
    height = -(-columns // 8) * 16
    pool_count = served_rows.size
    position = jnp.stack([lax.axis_index("dom"), lax.axis_index("col") & 1]).astype(I32)
    smem = pl.BlockSpec(memory_space=pltpu.SMEM)
    vmem = pl.BlockSpec(memory_space=pltpu.VMEM)
    anywhere = pl.BlockSpec(memory_space=pl.ANY)
    packet_rows = PACK + 2 * edges // LANES
    limit = VMEM_BASE + pool_count * VMEM_PER_POOL_ROW

    def local(kernel, out, *args, scratch=(), flops=0, grid=None, out_specs=None, specs=None):
        outs = out if isinstance(out, tuple) else (out,)
        chosen = [smem if a is position else vmem for a in args]
        for place, spec in (specs or {}).items():
            chosen[place] = spec
        extra = {} if grid is None else {"grid": grid}
        return pl.pallas_call(
            kernel,
            out_shape=out,
            in_specs=chosen,
            out_specs=jax.tree.map(lambda _: vmem, out) if out_specs is None else out_specs,
            scratch_shapes=list(scratch),
            compiler_params=pltpu.CompilerParams(vmem_limit_bytes=limit),
            cost_estimate=pl.CostEstimate(
                flops=int(flops),
                bytes_accessed=int(sum(a.size * a.dtype.itemsize for a in args + outs)),
                transcendentals=0,
            ),
            **extra,
        )(*args)

    edge_rows = struct(height, edges)
    gather_flops = 2 * LANES * entities * edges
    ids = jnp.concatenate(
        [source_ids, relation_ids, target_ids, jnp.pad(served_rows, ((0, 0), (0, edges - served_rows.shape[1])))],
        axis=0,
    )
    emb_lines, rel_lines = lines(embeddings), lines(relations)
    rel = local(
        relation_kernel, struct(height, relation_count), rel_lines, scratch=(pltpu.VMEM(rel_lines.shape, F32),)
    )
    emb, packet, served = local(
        functools.partial(prepare_kernel, buckets, served_rows.shape[1]),
        (struct(height, entities), struct(size, packet_rows, LANES), struct(1, pool_count, dtype=I32)),
        position, ids, emb_lines, rel,
        specs={3: anywhere},
        scratch=(
            pltpu.VMEM(emb_lines.shape, F32),
            pltpu.VMEM((buckets, packet_rows - PACK, LANES), BF16),
        ),
        flops=2 * LANES * entities * pool_count,
    )
    packet = lax.all_to_all(packet, "dom", split_axis=0, concat_axis=0, tiled=True)
    made = local(product_kernel, (edge_rows,) * (2 * buckets), emb, rel, ids, flops=gather_flops * buckets)
    products, relation_rows = made[:buckets], made[buckets:]
    last = buckets - 1

    def take_targets(chosen, *after):
        return local(
            functools.partial(target_kernel, chosen), (edge_rows,) * len(chosen), emb, asked, *after,
            specs={2 + k: anywhere for k in range(len(after))},
            flops=gather_flops * len(chosen),
        )

    owned_products = [products[0]] + [rotate(products[b], "dom", -b) for b in range(1, last)]
    width = buckets // 2 * edges
    pieces = 2
    piece = struct(pool_count, width // pieces)
    pool, asked, mine, *theirs = local(
        functools.partial(score_kernel, buckets),
        (
            struct(pool_count, LANES),
            struct(buckets, edges, dtype=I32),
            struct(pool_count, width, dtype=F32),
            *(piece,) * pieces,
        ),
        position, packet, ids, *products,
        flops=2 * LANES * pool_count * edges * buckets,
    )
    (last_target,) = take_targets((last,))
    last_target = rotate(last_target, "dom", last)
    pair = local(pair_kernel, (piece,) * pieces, mine, *[swap(part, "col", 1) for part in theirs])
    targets = [*take_targets(tuple(range(last))), last_target]
    home_cols, middle_cols, final_cols = local(
        columns_kernel,
        (
            struct((buckets + 1) * edges, LANES, dtype=I32),
            struct((last - 1) * edges, LANES, dtype=I32),
            struct(edges + pool_count, LANES, dtype=I32),
        ),
        ids, asked, served, targets[0],
        specs={3: anywhere},
    )
    after = [final_cols, *owned_products[1:], last_target]
    slopes_mine = local(
        functools.partial(slope_kernel, pieces), struct(pool_count, width),
        position, negative_ids, *pair, *[swap(part, "col", 2) for part in pair], *after,
        specs={2 + 2 * pieces + k: anywhere for k in range(len(after))},
    )
    slopes_theirs = swap(slopes_mine, "col", 1)
    pairs = [x for b in range(last) for x in (owned_products[b], targets[b])] + [products[last], last_target]
    own = local(positive_kernel, struct(PACK, edges), *pairs)
    near = swap(own, "col", 1)
    plan = None
    groups = [list(range(size // 2)), list(range(size // 2, size))]
    if size == 2 * buckets and columns + 4 <= height // 2:
        carriers = [*range(1, last), size - last]

        def left_of(hop):
            return sorted(set(range(1, size)) - set(carriers) - {(hop + c) % size for c in carriers})

        hop = min(range(1, size), key=lambda h: len(left_of(h)))
        plan = (tuple(carriers), hop, tuple(left_of(hop)))
        groups = [[0], carriers, [hop + c for c in carriers]] + [[way] for way in left_of(hop)]
    *sent, query = local(
        functools.partial(pool_grad_kernel, buckets, groups, plan is not None),
        tuple(struct(len(group), PACK, LANES) for group in groups)
        + (struct(height, buckets * edges, dtype=F32),),
        position, slopes_mine, slopes_theirs, pool, *products,
        scratch=(pltpu.VMEM((size, PACK, LANES), BF16),),
        flops=4 * LANES * pool_count * edges * buckets,
    )
    joined = local(
        join_kernel, struct(2, PACK, edges), own, near, query, specs={2: anywhere}
    )
    far = swap(joined, "col", 2)
    if plan is None:
        riders, direct = (), ()
        parts, origins = exchange(*sent, "dom")
    else:
        riders, origins = (sent[1], rotate(sent[2], "dom", hop)), None
        direct = [rotate(block, "dom", way) for way, block in zip(plan[2], sent[3:])]
    slope, *scaled = local(
        functools.partial(scale_kernel, buckets, columns, len(riders)),
        (struct(PACK, edges, dtype=F32),) + (edge_rows,) * (buckets + 1),
        own, near, far, *targets, products[last], *riders,
    )
    pulls = [rotate(scaled[b], "dom", b) for b in range(1, last)]
    push = rotate(scaled[buckets], "dom", -last)
    if plan is not None:
        parts = (*pulls, sent[0], *direct)
    count = (buckets + 1) * edges
    held = local(
        home_kernel,
        struct(height, entities, dtype=F32),
        ids, asked, slope, query, *owned_products, scaled[0], scaled[last], relation_rows[0], relation_rows[last], home_cols,
        scratch=(pltpu.VMEM((height, count), BF16),),
    )
    count = (last - 1) * edges
    held = local(
        middle_kernel,
        struct(height, entities, dtype=F32),
        ids, query, *relation_rows[1:last], *pulls, held, middle_cols,
        scratch=(pltpu.VMEM((height, count), BF16),),
        flops=2 * LANES * count * entities,
    )
    steps = 8
    count = edges + pool_count
    args = [position, asked, served, push, *parts, held, final_cols]
    grad = local(
        functools.partial(final_kernel, plan, origins),
        struct(columns, 2 * entities // LANES, LANES, dtype=F32),
        *args,
        out_specs=anywhere,
        scratch=(
            pltpu.VMEM((height, count), BF16),
            pltpu.VMEM((size, PACK, LANES), BF16),
            pltpu.VMEM((steps, columns, 2 * entities // LANES // steps, LANES), F32),
            pltpu.SemaphoreType.DMA((steps,)),
        ),
        flops=2 * LANES * count * entities,
    )
    return from_lines(grad, halves, columns, entities)


def solution(mesh):
    placed = (
        P(None, "col", "dom"),
        P(None, "col", None),
        P(None, "dom"),
        P(None, "dom"),
        P(None, "dom"),
        P(None, "dom", None),
        P("dom", None),
    )
    return jax.shard_map(
        body, mesh=mesh, in_specs=placed, out_specs=P(None, "col", "dom"), check_vma=False
    )
```
